256 devices in a mesh: rows: 16 (over z_lo, x, core), rep: 16 (over y, z_hi).
Axes of the slice: x: 4, y: 4, z: 8 (z_hi: 4, z_lo: 2; z = z_hi * 2 + z_lo), core: 2. Of those that a mesh axis runs over, the one named last changes fastest.
Arguments:
- node_features: bfloat16 [32768, 256], P(('rows', 'rep')), may hold values from -6 to 6
- adjacency: bfloat16 [256, 64, 128, 128], P('rows', 'rep'), may hold values from -0.078125 to 0.078125
- column_ids: int32 [256, 64], P('rows', 'rep'), may hold values from 0 to 15
- block_counts: int32 [256, 16], P('rows', 'rep'), may hold values from 1 to 4, 40 in all within a row
- weight_first: bfloat16 [256, 512], replicated, may hold values from -0.375 to 0.375
- weight_second: bfloat16 [512, 256], replicated, may hold values from -0.25 to 0.25
- cotangent: bfloat16 [32768, 256], P(('rows', 'rep')), may hold values from -6 to 6
Outputs:
- embedding: bfloat16 [32768, 256], P(('rows', 'rep'))
- grad_first: float32 [256, 512], replicated
- grad_second: float32 [512, 256], replicated
The draws below stay inside these ranges and needn't reach their ends.
Inputs may be any that keep to these rules, and one draw needn't show every extreme that they name: `block_counts`: each row block has 40 live slots over its 16 groups; some group of some row block has all 4 live.
All inputs are finite; a program needn't handle non-finite values.
Results may differ from the reference program's by a relative error of at most 0.024.
Values may be sent and summed in bfloat16 or wider, within the bound.
A program may use at most 64 MiB of HBM per device.

```python
import math
import jax
import jax.numpy as jnp
import numpy as np
from jax import lax

FIN = 256
HID = 512
OUT = 256
BS = 128
SLOTS = 4
BLK_DEV = 1
NBLK = 256
NODES = 32768
TOTAL = 40
N_ROWS = 16
N_REP = 16


def set_ends(array, own_key, low, top_value):
    index_at = [jax.random.randint(jax.random.fold_in(own_key, axis), (), 0, length) for axis, length in enumerate(array.shape)]
    main_axis = array.shape.index(max(array.shape))
    next_to = index_at[:main_axis] + [(index_at[main_axis] + 1) % array.shape[main_axis]] + index_at[main_axis + 1:]
    return array.at[tuple(index_at)].set(low).at[tuple(next_to)].set(top_value)


def steps_of(rng, dims, split, least, largest):
    def one(dim, shards_of):
        draws = jax.random.uniform(jax.random.fold_in(jax.random.fold_in(rng, 6), dim), (shards_of,), jnp.float32, least / len(split), largest / len(split))
        return jnp.repeat(jnp.exp(draws), dims[dim] // shards_of).reshape((-1,) + (1,) * (len(dims) - dim - 1))

    level = one(*split[0])
    for cut in split[1:]:
        level = level * one(*cut)
    return level


def length_profile(number_of, total, reach, skew):
    portions = [(1 << 20) // math.isqrt(rank ** skew) + 1 for rank in range(2, number_of + 1)]
    rest, holding = total - reach - (number_of - 1), [1] * (number_of - 1)
    while rest > 0:
        movable = [i for i in range(number_of - 1) if holding[i] < reach]
        whole, budget = sum([portions[i] for i in movable]), rest
        for i in movable:
            addition = min(reach - holding[i], max(1, budget * portions[i] // whole), rest)
            holding[i] = holding[i] + addition
            rest = rest - addition
    return np.array([reach] + holding)


def ragged(key, number_of, total, most, slope):
    if number_of == 2:
        one = jax.random.randint(key, (), max(1, total - most), min(most, total - 1) + 1)
        return jnp.stack([one, total - one])
    sizes = jnp.asarray(length_profile(number_of, total, most, slope), jnp.int32)
    couples = (number_of - 1) // 2
    giver, receiver = sizes[1:1 + 2 * couples:2], sizes[2:2 + 2 * couples:2]
    margin = jnp.minimum(giver - 1, most - receiver)
    shifted = jax.random.randint(jax.random.fold_in(key, 1), (couples,), 0, 1 << 20) % (margin + 1)
    sizes = sizes.at[1:1 + 2 * couples:2].set(giver - shifted).at[2:2 + 2 * couples:2].set(receiver + shifted)
    return sizes[jax.random.permutation(jax.random.fold_in(key, 2), number_of)]


def centred(rng, extent, width, most, split=(), kind=jnp.bfloat16):
    result = width * jax.random.normal(rng, extent, jnp.float32)
    if split:
        result = result * steps_of(rng, extent, split, -0.22, 0.18)
    return jnp.clip(result, -most, most).astype(kind)


def setup_inputs(seed: int = 0) -> dict:
    arg_keys = jax.random.split(jax.random.key(seed), 8)
    node_features = centred(arg_keys[0], (NODES, FIN), 1.0, 6.0, ((0, 256),))
    adjacency = centred(arg_keys[1], (NBLK, N_REP * SLOTS, BS, BS), (TOTAL * BS) ** -0.5, 0.078125, ((0, 16), (1, 16)))
    column_ids = set_ends(jax.random.randint(arg_keys[2], (NBLK, N_REP * SLOTS), 0, N_ROWS * BLK_DEV), jax.random.fold_in(arg_keys[2], 1), 0, (N_ROWS * BLK_DEV) - 1).astype(jnp.int32)
    block_counts = jax.vmap(lambda own: ragged(own, N_REP, TOTAL, SLOTS, 2))(jax.random.split(arg_keys[3], NBLK)).reshape((NBLK, N_REP)).astype(jnp.int32)
    weight_first = centred(arg_keys[4], (FIN, HID), FIN ** -0.5, 0.375)
    weight_second = centred(arg_keys[5], (HID, OUT), HID ** -0.5, 0.25)
    cotangent = centred(arg_keys[6], (NODES, OUT), 1.0, 6.0, ((0, 256),))
    return {"node_features": node_features, "adjacency": adjacency, "column_ids": column_ids, "block_counts": block_counts, "weight_first": weight_first, "weight_second": weight_second, "cotangent": cotangent}


def column_sets(node_field):
    feature_width = node_field.shape[1]
    shaped = node_field.reshape(N_ROWS, N_REP, BLK_DEV, BS, feature_width)
    return jnp.transpose(shaped, (1, 0, 2, 3, 4)).reshape(N_REP, N_ROWS * BLK_DEV, BS, feature_width)

def masked_blocks(adj_view, count_view, row_shard, rep_index):
    slot_index = jnp.arange(SLOTS, dtype=jnp.int32)
    blocks = adj_view[row_shard][:, rep_index].astype(jnp.float32)
    live_slots = slot_index[None, :] < count_view[row_shard][:, rep_index][:, None]
    return jnp.where(live_slots[:, :, None, None], blocks, jnp.zeros_like(blocks))

def aggregate(node_field, adjacency, column_ids, block_counts):
    feature_width = node_field.shape[1]
    gathered_sets = column_sets(node_field)
    row_blocks = BLK_DEV * N_REP
    adj_view = adjacency.reshape(N_ROWS, row_blocks, N_REP, SLOTS, BS, BS)
    id_view = column_ids.reshape(N_ROWS, row_blocks, N_REP, SLOTS)
    count_view = block_counts.reshape(N_ROWS, row_blocks, N_REP)

    def shard_rows(row_shard):

        def add_group(rep_index, running):
            blocks = masked_blocks(adj_view, count_view, row_shard, rep_index)
            picked = gathered_sets[rep_index][id_view[row_shard][:, rep_index]].astype(jnp.float32)
            partial_sum = jnp.einsum('rsij,rsjf->rif', blocks, picked)
            rounded = lax.optimization_barrier(partial_sum.astype(jnp.bfloat16))
            return running + rounded.astype(jnp.float32)
        return lax.fori_loop(0, N_REP, add_group, jnp.zeros((row_blocks, BS, feature_width), jnp.float32))
    stacked = lax.map(shard_rows, jnp.arange(N_ROWS, dtype=jnp.int32))
    return stacked.reshape(N_ROWS * row_blocks * BS, feature_width)

def transpose_aggregate(cotangent, adjacency, column_ids, block_counts):
    feature_width = cotangent.shape[1]
    row_blocks = BLK_DEV * N_REP
    col_blocks = N_ROWS * BLK_DEV
    grad_view = cotangent.reshape(N_ROWS, row_blocks, BS, feature_width)
    adj_view = adjacency.reshape(N_ROWS, row_blocks, N_REP, SLOTS, BS, BS)
    id_view = column_ids.reshape(N_ROWS, row_blocks, N_REP, SLOTS)
    count_view = block_counts.reshape(N_ROWS, row_blocks, N_REP)

    def add_device(device_index, running):
        row_shard = device_index // N_REP
        rep_index = device_index % N_REP
        blocks = masked_blocks(adj_view, count_view, row_shard, rep_index)
        terms = jnp.einsum('rsij,rif->rsjf', blocks, grad_view[row_shard].astype(jnp.float32))
        segment_ids = id_view[row_shard][:, rep_index].reshape(-1).astype(jnp.int32)
        summed = jax.ops.segment_sum(terms.reshape(row_blocks * SLOTS, BS, feature_width), segment_ids, num_segments=col_blocks)
        rounded = lax.optimization_barrier(summed.astype(jnp.bfloat16))
        return running.at[rep_index].add(rounded.astype(jnp.float32))
    running = lax.fori_loop(0, N_ROWS * N_REP, add_device, jnp.zeros((N_REP, col_blocks, BS, feature_width), jnp.float32))
    shaped = running.reshape(N_REP, N_ROWS, BLK_DEV, BS, feature_width)
    return jnp.transpose(shaped, (1, 0, 2, 3, 4)).reshape(NODES, feature_width)

def reference(node_features, adjacency, column_ids, block_counts, weight_first, weight_second, cotangent):
    contract = (((0,), (0,)), ((), ()))
    mixed_input = aggregate(node_features, adjacency, column_ids, block_counts).astype(jnp.bfloat16)
    pre_first = jnp.dot(mixed_input, weight_first, preferred_element_type=jnp.float32)
    hidden = jax.nn.silu(pre_first).astype(jnp.bfloat16)
    second_in = jnp.dot(hidden, weight_second, preferred_element_type=jnp.float32).astype(jnp.bfloat16)
    embedding = aggregate(second_in, adjacency, column_ids, block_counts).astype(jnp.bfloat16)
    upstream = transpose_aggregate(cotangent, adjacency, column_ids, block_counts).astype(jnp.bfloat16)
    scale_factor = 1.0 / math.sqrt(NODES)
    grad_second = lax.dot_general(hidden, upstream, contract, preferred_element_type=jnp.float32) * scale_factor
    back_hidden = lax.dot_general(upstream, weight_second, (((1,), (1,)), ((), ())), preferred_element_type=jnp.float32)
    sigmoid_gate = jax.nn.sigmoid(pre_first)
    back_pre = (back_hidden * sigmoid_gate * (1.0 + pre_first * (1.0 - sigmoid_gate))).astype(jnp.bfloat16)
    grad_first = lax.dot_general(mixed_input, back_pre, contract, preferred_element_type=jnp.float32) * scale_factor
    return (embedding, grad_first, grad_second)
```

```python
import functools
import math

import jax
import jax.numpy as jnp
from jax import lax
from jax.experimental import pallas as pl
from jax.experimental.pallas import tpu as pltpu
from jax.sharding import PartitionSpec as P

MESH = pl.DeviceIdType.MESH
F32 = jnp.float32
BF16 = jnp.bfloat16
NY = 4


def dot(a, b):
    return jnp.dot(a, b, preferred_element_type=F32)


def dot_dims(a, b, ca, cb):
    return lax.dot_general(a, b, (((ca,), (cb,)), ((), ())), preferred_element_type=F32)


def loop(lo, hi, body):
    def step(i, carry):
        body(i)
        return carry

    lax.fori_loop(lo, hi, step, 0)


def kernel(
    ny,
    scale,
    ids,
    counts,
    x_ref,
    adj_ref,
    w1_ref,
    w2_ref,
    cot_ref,
    emb_ref,
    g1_ref,
    g2_ref,
    dense,
    feat1,
    feat2,
    cotb,
    terms1,
    terms2,
    ybuf1,
    ybuf2,
    zsend1,
    zsend2,
    zrecv1,
    zrecv2,
    own_sum,
    second,
    tsend,
    trecv,
    town,
    tchip,
    mixed_s,
    hidden_s,
    pre_s,
    glocal,
    gsib,
    gchip,
    gchip_r,
    gtile,
    gtile_r,
    gall,
    gfin,
    gpiece,
    s_ag1,
    r_ag1,
    f_ag1,
    s_ag2,
    r_ag2,
    f_ag2,
    s_ag3,
    r_ag3,
    f_ag3,
    s_cot,
    rz_cot,
    ry_cot,
    s_rs1,
    ry_rs1,
    rz_rs1,
    s_rs2,
    ry_rs2,
    rz_rs2,
    s_t,
    rs_t,
    rc_t,
    s_g,
    rs_g,
    rc_g,
    rr_g,
    ra_g,
):
    rows = lax.axis_size("rows")
    rep = lax.axis_size("rep")
    nq = rows // 2
    nz = rep // ny
    bs = x_ref.shape[0]
    r = lax.axis_index("rows")
    c = lax.axis_index("rep")
    core = lax.rem(r, 2)
    q = r // 2
    y = c // nz
    z = lax.rem(c, nz)
    sib = r + 1 - 2 * core

    def chip_at(d):
        return lax.rem(q + d, nq)

    def chip_before(d):
        return lax.rem(q + nq - d, nq)

    def at_chip(q2):
        return (2 * q2 + core, c)

    def at_y(dy):
        y2 = lax.rem(y + dy, ny)
        return y2, (r, y2 * nz + z)

    def at_z(dz):
        z2 = lax.rem(z + dz, nz)
        return z2, (r, y * nz + z2)

    def send(src, dst, ssem, rsem, dev):
        pltpu.make_async_remote_copy(
            src_ref=src, dst_ref=dst, send_sem=ssem, recv_sem=rsem, device_id=dev, device_id_type=MESH
        ).start()

    def wait(ref, sem):
        pltpu.make_async_copy(ref, ref, sem).wait()

    barrier = pltpu.get_barrier_semaphore()
    pl.semaphore_signal(barrier, inc=1, device_id=(sib, c), device_id_type=MESH)
    loop(1, nq, lambda d: pl.semaphore_signal(barrier, inc=1, device_id=at_chip(chip_at(d)), device_id_type=MESH))
    loop(
        1,
        rep,
        lambda d: pl.semaphore_signal(
            barrier, inc=1, device_id=(r, lax.rem(c + d, rep)), device_id_type=MESH
        ),
    )
    pl.semaphore_wait(barrier, 1 + (nq - 1) + (rep - 1))

    def gather_start(src, buf, ssem, rsem, fsem):
        loop(1, nq, lambda d: send(src, buf.at[core, q], ssem.at[0], rsem.at[d - 1], at_chip(chip_at(d))))
        send(src, buf.at[core, q], ssem.at[0], fsem.at[0], (sib, c))

    def gather_pass(buf, ssem, rsem, fsem):
        def one(d):
            block = buf.at[core, chip_before(d)]
            wait(block, rsem.at[d - 1])
            send(block, block, ssem.at[1], fsem.at[0], (sib, c))

        loop(1, nq, one)

    def gather_end(buf, ssem, fsem):
        wait(buf.at[1 - core], fsem.at[0])

    def gather_sent(buf, ssem):
        wait(buf.at[0], ssem.at[0])
        wait(buf.at[0, pl.ds(0, nq - 1)], ssem.at[1])

    gather_start(x_ref, feat1, s_ag1, r_ag1, f_ag1)
    feat1[core, q] = x_ref[...]

    cotb[z, y] = cot_ref[...].astype(F32).T.astype(BF16)
    own_cot = cotb.at[z, y]
    for dz in range(1, nz):
        send(own_cot, own_cot, s_cot.at[0], rz_cot.at[dz - 1], at_z(dz)[1])
    for dy in range(1, ny):
        send(own_cot, own_cot, s_cot.at[1], ry_cot.at[0], at_y(dy)[1])

    def densify(b):
        z2 = lax.rem(b, nz)
        y2 = b // nz
        blocks = [adj_ref[b, s] for s in range(adj_ref.shape[1])]
        zero = jnp.zeros_like(blocks[0])
        where_to = [jnp.where(s < counts[b, 0], ids[b, s], -1) for s in range(len(blocks))]
        row = pl.ds(pl.multiple_of(y2 * bs, bs), bs)
        for p in range(rows):
            total = jnp.where(where_to[0] == p, blocks[0], zero)
            for s in range(1, len(blocks)):
                total = total + jnp.where(where_to[s] == p, blocks[s], zero)
            dense[p % 2, z2, row, (p // 2) * bs : (p // 2 + 1) * bs] = total

    loop(0, rep, densify)

    gather_pass(feat1, s_ag1, r_ag1, f_ag1)
    for dz in range(1, nz):
        z3 = lax.rem(z + nz - dz, nz)
        block = cotb.at[z3, y]
        wait(block, rz_cot.at[dz - 1])
        for dy in range(1, ny):
            send(block, block, s_cot.at[1], ry_cot.at[dz], at_y(dy)[1])
    gather_end(feat1, s_ag1, f_ag1)

    def aggregate_start(feat, terms, ybuf, ssem, rysem):
        def one(k):
            z2 = lax.rem(z + k + 1, nz)
            total = dot(dense[0, z2], feat[0].reshape(nq * bs, -1))
            total = total + dot(dense[1, z2], feat[1].reshape(nq * bs, -1))
            terms[z2] = total.astype(BF16).reshape(terms.shape[1:])
            for dy in range(1, ny):
                y2, dev = at_y(dy)
                send(terms.at[z2, y2], ybuf.at[k, dy - 1], ssem.at[0], rysem.at[k], dev)

        loop(0, nz, one)

    def aggregate_fold(k, terms, ybuf, zsend, zrecv, ssem, rysem, rzsem):
        z2, dev = at_z(k + 1)
        wait(ybuf.at[k], rysem.at[k])
        total = terms[z2, y].astype(F32)
        for i in range(ny - 1):
            total = total + ybuf[k, i].astype(F32)
        if k < nz - 1:
            zsend[k] = total.astype(BF16)
            send(zsend.at[k], zrecv.at[k], ssem.at[1], rzsem.at[0], dev)
        else:
            own_sum[...] = total

    def aggregate_end(zrecv, rzsem):
        wait(zrecv, rzsem.at[0])
        total = own_sum[...]
        for k in range(nz - 1):
            total = total + zrecv[k].astype(F32)
        return total

    def aggregate_sent(ybuf, zsend, ssem):
        wait(ybuf, ssem.at[0])
        wait(zsend, ssem.at[1])

    aggregate_start(feat1, terms1, ybuf1, s_rs1, ry_rs1)

    for k in range(nz):
        wait(ybuf1.at[0], ry_cot.at[k])

    two = 2 * bs

    def transposed_terms(par, n):
        col = pl.ds(pl.multiple_of(n * two, two), two)
        total = None
        for z2 in range(nz):
            left = jnp.concatenate([cotb[z2, y2] for y2 in range(ny)], axis=1)
            part = dot(left, dense[par, z2, :, col])
            total = part if total is None else total + part
        return total

    def t_other(n):
        total = transposed_terms(1 - core, n).astype(BF16)
        tsend[2 * n] = total[:, :bs]
        tsend[2 * n + 1] = total[:, bs:]
        pair = pl.ds(2 * n, 2)
        send(tsend.at[pair], trecv.at[pair], s_t.at[0], rs_t.at[n], (sib, c))

    loop(0, nq // 2, t_other)

    fold1 = functools.partial(
        aggregate_fold,
        terms=terms1,
        ybuf=ybuf1,
        zsend=zsend1,
        zrecv=zrecv1,
        ssem=s_rs1,
        rysem=ry_rs1,
        rzsem=rz_rs1,
    )
    fold1(0)

    def t_own(n):
        total = transposed_terms(core, n)
        wait(trecv.at[pl.ds(2 * n, 2)], rs_t.at[n])
        town[2 * n] = (total[:, :bs] + trecv[2 * n].astype(F32)).astype(BF16)
        town[2 * n + 1] = (total[:, bs:] + trecv[2 * n + 1].astype(F32)).astype(BF16)

    loop(0, nq // 2, t_own)
    fold1(1)
    loop(
        1,
        nq,
        lambda d: send(town.at[chip_at(d)], tchip.at[d - 1], s_t.at[1], rc_t.at[0], at_chip(chip_at(d))),
    )
    for k in range(2, nz):
        fold1(k)

    mixed = aggregate_end(zrecv1, rz_rs1).astype(BF16)
    mixed_s[...] = mixed
    pre = dot(mixed, w1_ref[...])
    pre_s[...] = pre
    hidden = (pre / (1.0 + jnp.exp(-pre))).astype(BF16)
    hidden_s[...] = hidden
    second[...] = dot(hidden, w2_ref[...]).astype(BF16)
    gather_start(second, feat2, s_ag2, r_ag2, f_ag2)
    feat2[core, q] = second[...]

    wait(tchip, rc_t.at[0])
    up = town[q].astype(F32)
    for d in range(nq - 1):
        up = up + tchip[d].astype(F32)
    up_t = up.astype(BF16)
    glocal[1] = (dot(up_t, hidden_s[...]) * scale).astype(BF16)
    back = dot_dims(up.T.astype(BF16), w2_ref[...], 1, 1)
    pre = pre_s[...]
    gate = 1.0 / (1.0 + jnp.exp(-pre))
    back_pre = (back * gate * (1.0 + pre * (1.0 - gate))).astype(BF16)
    glocal[0] = (dot_dims(mixed_s[...], back_pre, 0, 0) * scale).astype(BF16)
    send(glocal.at[1 - core], gsib, s_g.at[0], rs_g.at[0], (sib, c))

    gather_pass(feat2, s_ag2, r_ag2, f_ag2)

    wait(gsib, rs_g.at[0])
    gchip[...] = (glocal[core].astype(F32) + gsib[...].astype(F32)).astype(BF16).reshape(gchip.shape)
    loop(
        1,
        nq,
        lambda d: send(gchip.at[chip_at(d)], gchip_r.at[d - 1], s_g.at[1], rc_g.at[0], at_chip(chip_at(d))),
    )

    gather_end(feat2, s_ag2, f_ag2)
    aggregate_start(feat2, terms2, ybuf2, s_rs2, ry_rs2)
    fold2 = functools.partial(
        aggregate_fold,
        terms=terms2,
        ybuf=ybuf2,
        zsend=zsend2,
        zrecv=zrecv2,
        ssem=s_rs2,
        rysem=ry_rs2,
        rzsem=rz_rs2,
    )

    wait(gchip_r, rc_g.at[0])
    share = gchip[q].astype(F32)
    for d in range(nq - 1):
        share = share + gchip_r[d].astype(F32)
    tile_rows, tile_cols = gtile.shape[1:]
    across = share.shape[1] // tile_cols
    for t in range(rep):
        i, j = t // across, t % across
        gtile[t] = share[i * tile_rows : (i + 1) * tile_rows, j * tile_cols : (j + 1) * tile_cols]

    def at_rep(d):
        return lax.rem(c + d, rep)

    loop(1, rep, lambda d: send(gtile.at[at_rep(d)], gtile_r.at[d - 1], s_g.at[2], rr_g.at[0], (r, at_rep(d))))

    fold2(0)

    wait(gtile_r, rr_g.at[0])
    tile = gtile[c]
    for d in range(rep - 1):
        tile = tile + gtile_r[d]
    gall[c] = tile
    loop(1, rep, lambda d: send(gall.at[c], gall.at[c], s_g.at[3], ra_g.at[0], (r, at_rep(d))))

    fold2(1)

    wait(gtile_r, ra_g.at[0])
    for i in range(rep // across):
        strip = jnp.concatenate([gall[i * across + j] for j in range(across)], axis=1)
        gpiece[i * tile_rows : (i + 1) * tile_rows, :] = strip
    gfin[core, q] = gpiece[...].astype(BF16)
    own_piece = gfin.at[core, q]
    gather_start(own_piece, gfin, s_ag3, r_ag3, f_ag3)

    for k in range(2, nz):
        fold2(k)
    gather_pass(gfin, s_ag3, r_ag3, f_ag3)
    emb_ref[...] = aggregate_end(zrecv2, rz_rs2).astype(BF16)

    gather_end(gfin, s_ag3, f_ag3)
    g1_ref[...] = gfin[0].reshape(g1_ref.shape).astype(F32)
    g2_ref[...] = gfin[1].reshape(g2_ref.shape[::-1]).astype(F32).T

    gather_sent(feat1, s_ag1)
    gather_sent(feat2, s_ag2)
    gather_sent(gfin, s_ag3)
    wait(cotb.at[0, pl.ds(0, nz - 1)], s_cot.at[0])
    wait(terms1.at[:, pl.ds(0, ny - 1)], s_cot.at[1])
    aggregate_sent(ybuf1, zsend1, s_rs1)
    aggregate_sent(ybuf2, zsend2, s_rs2)
    wait(tsend, s_t.at[0])
    wait(tchip, s_t.at[1])
    wait(gsib, s_g.at[0])
    wait(gchip_r, s_g.at[1])
    wait(gtile_r, s_g.at[2])
    wait(gtile_r, s_g.at[3])


def shards(ny, nodes, node_features, adjacency, column_ids, block_counts, w1, w2, cotangent):
    rows, rep = lax.axis_size("rows"), lax.axis_size("rep")
    nq, nz = rows // 2, rep // ny
    bs, width = node_features.shape
    hid = w1.shape[1]
    block = (bs, width)
    turned = (width, bs)
    share = (width // nq, hid)
    tile = (8, 128)
    vmem = pl.BlockSpec(memory_space=pltpu.VMEM)
    smem = pl.BlockSpec(memory_space=pltpu.SMEM)
    v = pltpu.VMEM
    dma = pltpu.SemaphoreType.DMA
    scratch = [
        v((2, nz, ny * bs, nq * bs), BF16),
        v((2, nq) + block, BF16),
        v((2, nq) + block, BF16),
        v((nz, ny) + turned, BF16),
        v((nz, ny) + block, BF16),
        v((nz, ny) + block, BF16),
        v((nz, ny - 1) + block, BF16),
        v((nz, ny - 1) + block, BF16),
        v((nz - 1,) + block, BF16),
        v((nz - 1,) + block, BF16),
        v((nz - 1,) + block, BF16),
        v((nz - 1,) + block, BF16),
        v(block, F32),
        v(block, BF16),
        v((nq,) + turned, BF16),
        v((nq,) + turned, BF16),
        v((nq,) + turned, BF16),
        v((nq - 1,) + turned, BF16),
        v(block, BF16),
        v((bs, hid), BF16),
        v((bs, hid), F32),
        v((2, width, hid), BF16),
        v((width, hid), BF16),
        v((nq,) + share, BF16),
        v((nq - 1,) + share, BF16),
        v((rep,) + tile, F32),
        v((rep - 1,) + tile, F32),
        v((rep,) + tile, F32),
        v((2, nq) + share, BF16),
        v(share, F32),
    ]
    ag = [dma((2,)), dma((nq - 1,)), dma((1,))]
    rs = [dma((2,)), dma((nz,)), dma((1,))]
    scratch += ag + ag + ag
    scratch += [dma((2,)), dma((nz - 1,)), dma((nz,))]
    scratch += rs + rs
    scratch += [dma((2,)), dma((nq // 2,)), dma((1,))]
    scratch += [dma((4,)), dma((1,)), dma((1,)), dma((1,)), dma((1,))]
    return pl.pallas_call(
        functools.partial(kernel, ny, 1.0 / math.sqrt(nodes)),
        out_shape=(
            jax.ShapeDtypeStruct(block, BF16),
            jax.ShapeDtypeStruct((width, hid), F32),
            jax.ShapeDtypeStruct((hid, width), F32),
        ),
        in_specs=[smem, smem, vmem, vmem, vmem, vmem, vmem],
        out_specs=(vmem, vmem, vmem),
        scratch_shapes=scratch,
        compiler_params=pltpu.CompilerParams(
            collective_id=0, has_side_effects=True, vmem_limit_bytes=48 * 1024 * 1024
        ),
        name="graph_step",
    )(column_ids, block_counts, node_features, adjacency, w1, w2, cotangent)


def build(mesh, ny):
    in_specs = (
        P(("rows", "rep"), None),
        P("rows", "rep", None, None),
        P("rows", "rep"),
        P("rows", "rep"),
        P(),
        P(),
        P(("rows", "rep"), None),
    )
    out_specs = (P(("rows", "rep"), None), P(), P())

    def run(node_features, *rest):
        body = functools.partial(shards, ny, node_features.shape[0])
        return jax.shard_map(
            body, mesh=mesh, in_specs=in_specs, out_specs=out_specs, check_vma=False
        )(node_features, *rest)

    return run


def solution(mesh):
    return build(mesh, NY)
```

```python
import functools
import math

import jax
import jax.numpy as jnp
from jax import lax
from jax.experimental import pallas as pl
from jax.experimental.pallas import tpu as pltpu
from jax.sharding import PartitionSpec as P

MESH = pl.DeviceIdType.MESH
F32 = jnp.float32
BF16 = jnp.bfloat16
VMEM_BYTES = 63 * 1024 * 1024
NL, NX, NY, NZ = 2, 4, 4, 4


def dot(a, b):
    return jnp.dot(a, b, preferred_element_type=F32)


def dot_dims(a, b, ca, cb):
    return lax.dot_general(a, b, (((ca,), (cb,)), ((), ())), preferred_element_type=F32)


def loop(lo, hi, body):
    def step(i, carry):
        body(i)
        return carry

    lax.fori_loop(lo, hi, step, 0)


def kernel(
    scale,
    ids,
    counts,
    x_hbm,
    adj_hbm,
    w1_hbm,
    w2_hbm,
    cot_hbm,
    emb_ref,
    g1_ref,
    g2_ref,
    adj_ref,
    w1_ref,
    w2_ref,
    cot_ref,
    dense,
    feat1,
    feat2,
    cotb,
    terms1,
    terms2,
    hop1,
    hop2,
    ybuf1,
    ybuf2,
    zsend1,
    zsend2,
    zrecv1,
    zrecv2,
    own_sum,
    second,
    tsend,
    trecv,
    town,
    tchip,
    mixed_s,
    hidden_s,
    pre_s,
    glocal,
    gsib,
    gplane,
    gplane_r,
    gline,
    gfin,
    near2,
    near3,
    s_ag1,
    r_ag1,
    f_ag1,
    s_ag2,
    r_ag2,
    f_ag2,
    s_cot,
    rz_cot,
    ry_cot,
    s_rs1,
    rh_rs1,
    ry_rs1,
    rz_rs1,
    s_rs2,
    rh_rs2,
    ry_rs2,
    rz_rs2,
    s_t,
    rs_t,
    rc_t,
    s_g,
    rs_g,
    rp_g,
    rl_g,
    ra_g,
    rf_g,
    s_in,
):
    rows, rep = 2 * NL * NX, NY * NZ
    nq = NL * NX
    bs = x_hbm.shape[0]
    half = bs // 2
    r = lax.axis_index("rows")
    c = lax.axis_index("rep")
    core = lax.rem(r, 2)
    q = r // 2
    l = q // NX
    x = lax.rem(q, NX)
    y = c // NZ
    z = lax.rem(c, NZ)
    sib = (r + 1 - 2 * core, c)

    def xs(d):
        return lax.rem(x + d, NX)

    def ys(d):
        return lax.rem(y + d, NY)

    def zs(d):
        return lax.rem(z + d, NZ)

    def dev(l2=l, x2=x, y2=y, z2=z):
        return ((l2 * NX + x2) * 2 + core, y2 * NZ + z2)

    def chip_at(d):
        return lax.rem(q + d, nq)

    def send(src, dst, ssem, rsem, device):
        pltpu.make_async_remote_copy(
            src_ref=src, dst_ref=dst, send_sem=ssem, recv_sem=rsem, device_id=device, device_id_type=MESH
        ).start()

    def wait(ref, sem):
        pltpu.make_async_copy(ref, ref, sem).wait()

    near = [
        sib,
        dev(l2=1 - l),
        dev(x2=xs(1)),
        dev(x2=xs(2)),
        dev(x2=xs(3)),
        dev(y2=ys(1)),
        dev(y2=ys(3)),
        dev(z2=zs(1)),
        dev(z2=zs(3)),
    ]

    def greet(sem):
        for device in near:
            pl.semaphore_signal(sem, inc=1, device_id=device, device_id_type=MESH)

    def greeted(sem):
        pl.semaphore_wait(sem, len(near))

    barrier = pltpu.get_barrier_semaphore()
    greet(barrier)
    fetch = [
        pltpu.make_async_copy(src, dst, s_in.at[i])
        for i, (src, dst) in enumerate(
            [
                (cot_hbm, cot_ref),
                (x_hbm, feat1.at[core, q]),
                (adj_hbm, adj_ref),
                (w1_hbm, w1_ref),
                (w2_hbm, w2_ref),
            ]
        )
    ]
    for copy in fetch:
        copy.start()

    def gather_start(src, buf, ssem, rsem, fsem):
        to = buf.at[core, q]
        for i, device in enumerate([dev(l2=1 - l), dev(x2=xs(2)), dev(x2=xs(1)), dev(x2=xs(3))]):
            send(src, to, ssem.at[0], rsem.at[i], device)
        send(src, to, ssem.at[0], fsem.at[0], sib)

    def gather_pass(buf, ssem, rsem, fsem, steps):
        there = 1 - l
        came = [
            (there, x, [(4, dev(x2=xs(1))), (5, dev(x2=xs(3)))]),
            (l, xs(2), [(6, dev(l2=there))]),
            (l, xs(3), []),
            (l, xs(1), []),
            (there, xs(3), []),
            (there, xs(1), []),
            (there, xs(2), []),
        ]
        for i in steps:
            l2, x2, onward = came[i]
            block = buf.at[core, l2 * NX + x2]
            wait(block, rsem.at[i])
            for j, device in onward:
                send(block, block, ssem.at[0], rsem.at[j], device)
            send(block, block, ssem.at[1], fsem.at[0], sib)

    def gather_end(buf, fsem):
        wait(buf.at[1 - core], fsem.at[0])

    def gather_sent(buf, ssem):
        wait(buf.at[0], ssem.at[0])
        wait(buf.at[0, pl.ds(0, nq - 1)], ssem.at[1])

    def cot_turn():
        fetch[0].wait()
        cotb[z, y] = cot_ref[...].astype(F32).T.astype(BF16)

    def cot_z(dz):
        own = cotb.at[z, y]
        send(own, own, s_cot.at[0], rz_cot.at[dz - 1], dev(z2=zs(dz)))

    def cot_y(dz):
        block = cotb.at[zs(NZ - dz), y]
        if dz > 0:
            wait(block, rz_cot.at[dz - 1])
        for side, dy in ((0, 1), (1, 3)):
            send(block, block, s_cot.at[1], ry_cot.at[dz, side], dev(y2=ys(dy)))

    def cot_on(dz):
        for side, dy, rows_of in ((0, 1, pl.ds(0, width // 2)), (1, 3, pl.ds(width // 2, width // 2))):
            block = cotb.at[zs(NZ - dz), ys(4 - dy)]
            wait(block, ry_cot.at[dz, side])
            part = block.at[rows_of]
            send(part, part, s_cot.at[1], ry_cot.at[dz, 2], dev(y2=ys(dy)))

    def cot_end():
        for dz in range(NZ):
            wait(cotb.at[zs(NZ - dz), ys(2)], ry_cot.at[dz, 2])

    def cot_sent():
        wait(cotb.at[0, pl.ds(0, NZ - 1)], s_cot.at[0])
        wait(cotb.at[:, pl.ds(0, 3)], s_cot.at[1])

    width = x_hbm.shape[1]

    def densify(b):
        z2 = lax.rem(b, NZ)
        y2 = b // NZ
        blocks = [adj_ref[b, s] for s in range(adj_ref.shape[1])]
        zero = jnp.zeros_like(blocks[0])
        where_to = [jnp.where(s < counts[0, b], ids[s, b], -1) for s in range(len(blocks))]
        row = pl.ds(pl.multiple_of(y2 * bs, bs), bs)
        for p in range(rows):
            total = jnp.where(where_to[0] == p, blocks[0], zero)
            for s in range(1, len(blocks)):
                total = total + jnp.where(where_to[s] == p, blocks[s], zero)
            dense[p % 2, z2, row, (p // 2) * bs : (p // 2 + 1) * bs] = total

    def aggregate_start(feat, terms, hop, ssem, rhsem):
        def one(k):
            z2 = lax.rem(z + k + 1, NZ)
            total = dot(dense[0, z2], feat[0].reshape(nq * bs, -1))
            total = total + dot(dense[1, z2], feat[1].reshape(nq * bs, -1))
            terms[z2] = total.astype(BF16).reshape(terms.shape[1:])
            for side, dy in ((0, 1), (1, 3)):
                part = terms.at[z2, ys(2), pl.ds(side * half, half)]
                send(part, hop.at[k, side], ssem.at[0], rhsem.at[k], dev(y2=ys(dy)))

        loop(0, NZ, one)

    def aggregate_on(k, terms, hop, ybuf, ssem, rhsem, rysem):
        z2 = zs(k + 1)
        wait(hop.at[k], rhsem.at[k])
        for side, dy in ((0, 1), (1, 3)):
            y2 = ys(dy)
            at = pl.ds(side * half, half)
            both = terms[z2, y2, at].astype(F32) + hop[k, side].astype(F32)
            terms[z2, y2, at] = both.astype(BF16)
            send(terms.at[z2, y2], ybuf.at[k, side], ssem.at[0], rysem.at[k], dev(y2=y2))

    def aggregate_fold(k, terms, ybuf, zsend, zrecv, ssem, rysem, rzsem):
        wait(ybuf.at[k], rysem.at[k])
        total = terms[zs(k + 1), y].astype(F32) + ybuf[k, 0].astype(F32) + ybuf[k, 1].astype(F32)
        if k < NZ - 1:
            zsend[k] = total.astype(BF16)
            send(zsend.at[k], zrecv.at[k], ssem.at[1], rzsem.at[0], dev(z2=zs(k + 1)))
        else:
            own_sum[...] = total

    def aggregate_end(zrecv, rzsem):
        wait(zrecv, rzsem.at[0])
        total = own_sum[...]
        for k in range(NZ - 1):
            total = total + zrecv[k].astype(F32)
        return total

    def aggregate_sent(terms, zsend, ssem):
        wait(terms.at[:, pl.ds(0, 3)], ssem.at[0])
        wait(zsend, ssem.at[1])

    def on1(k):
        aggregate_on(k, terms1, hop1, ybuf1, s_rs1, rh_rs1, ry_rs1)

    def on2(k):
        aggregate_on(k, terms2, hop2, ybuf2, s_rs2, rh_rs2, ry_rs2)

    def fold1(k):
        aggregate_fold(k, terms1, ybuf1, zsend1, zrecv1, s_rs1, ry_rs1, rz_rs1)

    def fold2(k):
        aggregate_fold(k, terms2, ybuf2, zsend2, zrecv2, s_rs2, ry_rs2, rz_rs2)

    two = 2 * bs

    def transposed_terms(par, n):
        col = pl.ds(pl.multiple_of(n * two, two), two)
        total = None
        for z2 in range(NZ):
            left = jnp.concatenate([cotb[z2, y2] for y2 in range(NY)], axis=1)
            part = dot(left, dense[par, z2, :, col])
            total = part if total is None else total + part
        return total

    def t_other(n):
        total = transposed_terms(1 - core, n).astype(BF16)
        tsend[2 * n] = total[:, :bs]
        tsend[2 * n + 1] = total[:, bs:]
        pair = pl.ds(2 * n, 2)
        send(tsend.at[pair], trecv.at[pair], s_t.at[0], rs_t.at[n], sib)

    def t_own(n):
        total = transposed_terms(core, n)
        wait(trecv.at[pl.ds(2 * n, 2)], rs_t.at[n])
        town[2 * n] = (total[:, :bs] + trecv[2 * n].astype(F32)).astype(BF16)
        town[2 * n + 1] = (total[:, bs:] + trecv[2 * n + 1].astype(F32)).astype(BF16)

    def t_chips():
        def one(d):
            q2 = chip_at(d)
            send(town.at[q2], tchip.at[d - 1], s_t.at[1], rc_t.at[0], (2 * q2 + core, c))

        loop(1, nq, one)

    def t_sent():
        wait(tsend, s_t.at[0])
        wait(tchip, s_t.at[1])

    def first_layer():
        mixed = aggregate_end(zrecv1, rz_rs1).astype(BF16)
        mixed_s[...] = mixed
        pre = dot(mixed, w1_ref[...])
        pre_s[...] = pre
        hidden = (pre / (1.0 + jnp.exp(-pre))).astype(BF16)
        hidden_s[...] = hidden
        second[...] = dot(hidden, w2_ref[...]).astype(BF16)
        gather_start(second, feat2, s_ag2, r_ag2, f_ag2)
        feat2[core, q] = second[...]

    def gradients():
        wait(tchip, rc_t.at[0])
        up = town[q].astype(F32)
        for d in range(nq - 1):
            up = up + tchip[d].astype(F32)
        up = up.T.astype(BF16)
        second_grad = dot_dims(hidden_s[...], up, 0, 0) * scale
        glocal[1] = jnp.concatenate([second_grad[:width], second_grad[width:]], axis=1).astype(BF16)
        back = dot_dims(up, w2_ref[...], 1, 1)
        pre = pre_s[...]
        gate = 1.0 / (1.0 + jnp.exp(-pre))
        back_pre = (back * gate * (1.0 + pre * (1.0 - gate))).astype(BF16)
        glocal[0] = (dot_dims(mixed_s[...], back_pre, 0, 0) * scale).astype(BF16)
        send(glocal.at[1 - core], gsib, s_g.at[0], rs_g.at[0], sib)

    share = gplane.shape[1]
    place = x * NY + y

    def in_plane(d):
        m = lax.rem(place + d, NX * NY)
        return m, dev(x2=m // NY, y2=lax.rem(m, NY))

    def g_plane():
        wait(gsib, rs_g.at[0])
        both = glocal[core].astype(F32) + gsib[...].astype(F32)
        gplane[...] = both.astype(BF16).reshape(gplane.shape)

        def one(d):
            m, device = in_plane(d)
            send(gplane.at[m], gplane_r.at[d - 1], s_g.at[1], rp_g.at[0], device)

        loop(1, NX * NY, one)

    line = z * NL + l

    def g_line():
        wait(gplane_r, rp_g.at[0])
        total = gplane[place].astype(F32)
        for d in range(NX * NY - 1):
            total = total + gplane_r[d].astype(F32)
        gline[line] = total.astype(BF16)
        own = gline.at[line]

        def one(d):
            there = lax.rem(line + d, NZ * NL)
            send(own, own, s_g.at[2], rl_g.at[0], dev(l2=lax.rem(there, NL), z2=there // NL))

        loop(1, NZ * NL, one)

    def g_gather():
        wait(gline.at[pl.ds(0, NZ * NL - 1)], rl_g.at[0])
        total = gline[0].astype(F32)
        for i in range(1, NZ * NL):
            total = total + gline[i].astype(F32)
        gfin[core, place] = total.astype(BF16)
        own = gfin.at[core, place]
        loop(1, NX * NY, lambda d: send(own, own, s_g.at[3], ra_g.at[0], in_plane(d)[1]))

    def g_core():
        wait(gplane_r, ra_g.at[0])
        send(gfin.at[core], gfin.at[core], s_g.at[4], rf_g.at[0], sib)

    def g_out():
        wait(gfin.at[1 - core], rf_g.at[0])
        g1_ref[...] = gfin[0].reshape(g1_ref.shape).astype(F32)
        second_grad = gfin[1].reshape(g1_ref.shape).astype(F32)
        g2_ref[:width] = second_grad[:, : second_grad.shape[1] // 2]
        g2_ref[width:] = second_grad[:, second_grad.shape[1] // 2 :]

    def g_sent():
        wait(gsib, s_g.at[0])
        wait(gplane_r, s_g.at[1])
        wait(gline.at[pl.ds(0, NZ * NL - 1)], s_g.at[2])
        wait(gplane_r, s_g.at[3])
        wait(gfin.at[0], s_g.at[4])

    cot_turn()
    greeted(barrier)
    greet(near2)
    gather_start(x_hbm, feat1, s_ag1, r_ag1, f_ag1)
    cot_z(1)
    cot_z(3)
    cot_y(0)
    fetch[2].wait()
    loop(0, rep // 2, densify)
    greeted(near2)
    greet(near3)
    cot_z(2)
    gather_pass(feat1, s_ag1, r_ag1, f_ag1, [0])
    cot_y(1)
    cot_y(3)
    gather_pass(feat1, s_ag1, r_ag1, f_ag1, [1])
    loop(rep // 2, rep, densify)
    gather_pass(feat1, s_ag1, r_ag1, f_ag1, range(2, 7))
    cot_y(2)
    cot_on(0)
    fetch[1].wait()
    gather_end(feat1, f_ag1)
    aggregate_start(feat1, terms1, hop1, s_rs1, rh_rs1)
    cot_on(1)
    cot_on(3)
    loop(0, NZ, on1)
    cot_on(2)
    cot_end()
    loop(0, nq // 2, t_other)
    fold1(0)
    loop(0, nq // 2, t_own)
    fold1(1)
    t_chips()
    fold1(2)
    fold1(3)
    greeted(near3)
    fetch[3].wait()
    fetch[4].wait()
    first_layer()
    gradients()
    gather_pass(feat2, s_ag2, r_ag2, f_ag2, [0, 1])
    g_plane()
    gather_pass(feat2, s_ag2, r_ag2, f_ag2, range(2, 7))
    gather_end(feat2, f_ag2)
    aggregate_start(feat2, terms2, hop2, s_rs2, rh_rs2)
    g_line()
    loop(0, NZ, on2)
    fold2(0)
    g_gather()
    fold2(1)
    fold2(2)
    fold2(3)
    g_core()
    emb_ref[...] = aggregate_end(zrecv2, rz_rs2).astype(BF16)
    g_out()

    gather_sent(feat1, s_ag1)
    cot_sent()
    aggregate_sent(terms1, zsend1, s_rs1)
    gather_sent(feat2, s_ag2)
    aggregate_sent(terms2, zsend2, s_rs2)
    t_sent()
    g_sent()


def shards(nodes, node_features, adjacency, column_ids, block_counts, w1, w2, cotangent):
    rep, nq = NY * NZ, NL * NX
    bs, width = node_features.shape
    hid = w1.shape[1]
    block = (bs, width)
    turned = (width, bs)
    share = (width // (NX * NY), hid)
    vmem = pl.BlockSpec(memory_space=pltpu.VMEM)
    smem = pl.BlockSpec(memory_space=pltpu.SMEM)
    hbm = pl.BlockSpec(memory_space=pl.ANY)
    v = pltpu.VMEM
    dma = pltpu.SemaphoreType.DMA
    scratch = [
        v(adjacency.shape, BF16),
        v(w1.shape, BF16),
        v(w2.shape, BF16),
        v(block, BF16),
        v((2, NZ, NY * bs, nq * bs), BF16),
        v((2, nq) + block, BF16),
        v((2, nq) + block, BF16),
        v((NZ, NY) + turned, BF16),
        v((NZ, NY) + block, BF16),
        v((NZ, NY) + block, BF16),
        v((NZ, 2, bs // 2, width), BF16),
        v((NZ, 2, bs // 2, width), BF16),
        v((NZ, 2) + block, BF16),
        v((NZ, 2) + block, BF16),
        v((NZ - 1,) + block, BF16),
        v((NZ - 1,) + block, BF16),
        v((NZ - 1,) + block, BF16),
        v((NZ - 1,) + block, BF16),
        v(block, F32),
        v(block, BF16),
        v((nq,) + turned, BF16),
        v((nq,) + turned, BF16),
        v((nq,) + turned, BF16),
        v((nq - 1,) + turned, BF16),
        v(block, BF16),
        v((bs, hid), BF16),
        v((bs, hid), F32),
        v((2, width, hid), BF16),
        v((width, hid), BF16),
        v((NX * NY,) + share, BF16),
        v((NX * NY - 1,) + share, BF16),
        v((NZ * NL,) + share, BF16),
        v((2, NX * NY) + share, BF16),
        pltpu.SemaphoreType.REGULAR,
        pltpu.SemaphoreType.REGULAR,
    ]
    ag = [dma((2,)), dma((7,)), dma((1,))]
    rs = [dma((2,)), dma((NZ,)), dma((NZ,)), dma((1,))]
    scratch += ag + ag
    scratch += [dma((2,)), dma((NZ - 1,)), dma((NZ, 3))]
    scratch += rs + rs
    scratch += [dma((2,)), dma((nq // 2,)), dma((1,))]
    scratch += [dma((5,)), dma((1,)), dma((1,)), dma((1,)), dma((1,)), dma((1,)), dma((5,))]
    return pl.pallas_call(
        functools.partial(kernel, 1.0 / math.sqrt(nodes)),
        out_shape=(
            jax.ShapeDtypeStruct(block, BF16),
            jax.ShapeDtypeStruct((width, hid), F32),
            jax.ShapeDtypeStruct((hid, width), F32),
        ),
        in_specs=[smem, smem, hbm, hbm, hbm, hbm, hbm],
        out_specs=(vmem, vmem, vmem),
        scratch_shapes=scratch,
        compiler_params=pltpu.CompilerParams(
            collective_id=0, has_side_effects=True, vmem_limit_bytes=VMEM_BYTES
        ),
        name="graph_step",
    )(column_ids.T, block_counts.T, node_features, adjacency, w1, w2, cotangent)


def solution(mesh):
    in_specs = (
        P(("rows", "rep"), None),
        P("rows", "rep", None, None),
        P("rows", "rep"),
        P("rows", "rep"),
        P(),
        P(),
        P(("rows", "rep"), None),
    )
    out_specs = (P(("rows", "rep"), None), P(), P())

    def run(node_features, *rest):
        body = functools.partial(shards, node_features.shape[0])
        return jax.shard_map(
            body, mesh=mesh, in_specs=in_specs, out_specs=out_specs, check_vma=False
        )(node_features, *rest)

    return run
```

```python
import functools
import math

import jax
import jax.numpy as jnp
from jax import lax
from jax.experimental import pallas as pl
from jax.experimental.pallas import tpu as pltpu
from jax.sharding import PartitionSpec as P

MESH = pl.DeviceIdType.MESH
F32 = jnp.float32
BF16 = jnp.bfloat16
VMEM_BYTES = 63 * 1024 * 1024
NL, NX, NY, NZ = 2, 4, 4, 4
AHEAD = 2


def dot(a, b):
    return jnp.dot(a, b, preferred_element_type=F32)


def dot_dims(a, b, ca, cb):
    return lax.dot_general(a, b, (((ca,), (cb,)), ((), ())), preferred_element_type=F32)


def loop(lo, hi, body):
    def step(i, carry):
        body(i)
        return carry

    lax.fori_loop(lo, hi, step, 0)


def kernel(
    scale,
    ids,
    counts,
    x_hbm,
    adj_hbm,
    w1_hbm,
    w2_hbm,
    cot_hbm,
    emb_hbm,
    g_hbm,
    adj_ref,
    w1_ref,
    w2_ref,
    cot_ref,
    dense,
    feat1,
    feat2,
    cotb,
    terms1,
    terms2,
    hop1,
    hop2,
    ybuf1,
    ybuf2,
    zsend1,
    zsend2,
    zrecv1,
    zrecv2,
    own_sum,
    second,
    emb_s,
    tsend,
    trecv,
    town,
    tchip,
    mixed_s,
    hidden_s,
    pre_s,
    glocal,
    gsib,
    gplane,
    gplane_r,
    gline,
    gfin,
    near2,
    near3,
    s_ag1,
    r_ag1,
    f_ag1,
    s_ag2,
    r_ag2,
    f_ag2,
    s_cot,
    rz_cot,
    ry_cot,
    s_rs1,
    rh_rs1,
    ry_rs1,
    rz_rs1,
    s_rs2,
    rh_rs2,
    ry_rs2,
    rz_rs2,
    s_t,
    rs_t,
    rc_t,
    s_g,
    rs_g,
    rp_g,
    rl_g,
    ra_g,
    rf_g,
    s_in,
    s_out,
):
    rows, rep = 2 * NL * NX, NY * NZ
    nq = NL * NX
    bs = x_hbm.shape[0]
    half = bs // 2
    r = lax.axis_index("rows")
    c = lax.axis_index("rep")
    core = lax.rem(r, 2)
    q = r // 2
    l = q // NX
    x = lax.rem(q, NX)
    y = c // NZ
    z = lax.rem(c, NZ)
    sib = (r + 1 - 2 * core, c)

    def xs(d):
        return lax.rem(x + d, NX)

    def ys(d):
        return lax.rem(y + d, NY)

    def zs(d):
        return lax.rem(z + d, NZ)

    def dev(l2=l, x2=x, y2=y, z2=z):
        return ((l2 * NX + x2) * 2 + core, y2 * NZ + z2)

    def chip_at(d):
        return lax.rem(q + d, nq)

    def send(src, dst, ssem, rsem, device):
        pltpu.make_async_remote_copy(
            src_ref=src, dst_ref=dst, send_sem=ssem, recv_sem=rsem, device_id=device, device_id_type=MESH
        ).start()

    def wait(ref, sem):
        pltpu.make_async_copy(ref, ref, sem).wait()

    near = [
        sib,
        dev(l2=1 - l),
        dev(x2=xs(1)),
        dev(x2=xs(2)),
        dev(x2=xs(3)),
        dev(y2=ys(1)),
        dev(y2=ys(3)),
        dev(z2=zs(1)),
        dev(z2=zs(3)),
    ]

    def greet(sem):
        for device in near:
            pl.semaphore_signal(sem, inc=1, device_id=device, device_id_type=MESH)

    def greeted(sem):
        pl.semaphore_wait(sem, len(near))

    barrier = pltpu.get_barrier_semaphore()
    greet(barrier)
    emb_out = pltpu.make_async_copy(emb_s, emb_hbm, s_out.at[0])
    g_own_out = pltpu.make_async_copy(gfin.at[core], g_hbm.at[core], s_out.at[1])
    g_sib_out = pltpu.make_async_copy(gfin.at[1 - core], g_hbm.at[1 - core], s_out.at[2])
    fetch = [
        pltpu.make_async_copy(src, dst, s_in.at[i])
        for i, (src, dst) in enumerate(
            [
                (cot_hbm, cot_ref),
                (x_hbm, feat1.at[core, q]),
                (adj_hbm, adj_ref),
                (w1_hbm, w1_ref),
                (w2_hbm, w2_ref),
            ]
        )
    ]
    for copy in fetch:
        copy.start()

    def gather_start(src, buf, ssem, rsem, fsem):
        to = buf.at[core, q]
        for i, device in enumerate([dev(l2=1 - l), dev(x2=xs(2)), dev(x2=xs(1)), dev(x2=xs(3))]):
            send(src, to, ssem.at[0], rsem.at[i], device)
        send(src, to, ssem.at[0], fsem.at[0], sib)

    def gather_pass(buf, ssem, rsem, fsem, steps):
        there = 1 - l
        came = [
            (there, x, [(4, dev(x2=xs(1))), (5, dev(x2=xs(3)))]),
            (l, xs(2), [(6, dev(l2=there))]),
            (l, xs(3), []),
            (l, xs(1), []),
            (there, xs(3), []),
            (there, xs(1), []),
            (there, xs(2), []),
        ]
        for i in steps:
            l2, x2, onward = came[i]
            block = buf.at[core, l2 * NX + x2]
            wait(block, rsem.at[i])
            for j, device in onward:
                send(block, block, ssem.at[0], rsem.at[j], device)
            send(block, block, ssem.at[1], fsem.at[0], sib)

    def gather_end(buf, fsem):
        wait(buf.at[1 - core], fsem.at[0])

    def gather_sent(buf, ssem):
        wait(buf.at[0], ssem.at[0])
        wait(buf.at[0, pl.ds(0, nq - 1)], ssem.at[1])

    def cot_turn():
        fetch[0].wait()
        cotb[z, y] = cot_ref[...].astype(F32).T.astype(BF16)

    def cot_z(dz):
        own = cotb.at[z, y]
        send(own, own, s_cot.at[0], rz_cot.at[dz - 1], dev(z2=zs(dz)))

    def cot_y(dz):
        block = cotb.at[zs(NZ - dz), y]
        if dz > 0:
            wait(block, rz_cot.at[dz - 1])
        for side, dy in ((0, 1), (1, 3)):
            send(block, block, s_cot.at[1], ry_cot.at[dz, side], dev(y2=ys(dy)))

    def cot_on(dz):
        for side, dy, rows_of in ((0, 1, pl.ds(0, width // 2)), (1, 3, pl.ds(width // 2, width // 2))):
            block = cotb.at[zs(NZ - dz), ys(4 - dy)]
            wait(block, ry_cot.at[dz, side])
            part = block.at[rows_of]
            send(part, part, s_cot.at[1], ry_cot.at[dz, 2], dev(y2=ys(dy)))

    def cot_end():
        for dz in range(NZ):
            wait(cotb.at[zs(NZ - dz), ys(2)], ry_cot.at[dz, 2])

    def cot_sent():
        wait(cotb.at[0, pl.ds(0, NZ - 1)], s_cot.at[0])
        wait(cotb.at[:, pl.ds(0, 3)], s_cot.at[1])

    width = x_hbm.shape[1]

    def densify(b):
        z2 = lax.rem(b, NZ)
        y2 = b // NZ
        blocks = [adj_ref[b, s] for s in range(adj_ref.shape[1])]
        zero = jnp.zeros_like(blocks[0])
        where_to = [jnp.where(s < counts[0, b], ids[s, b], -1) for s in range(len(blocks))]
        row = pl.ds(pl.multiple_of(z2 * bs, bs), bs)
        for p in range(rows):
            total = jnp.where(where_to[0] == p, blocks[0], zero)
            for s in range(1, len(blocks)):
                total = total + jnp.where(where_to[s] == p, blocks[s], zero)
            dense[p % 2, y2, row, (p // 2) * bs : (p // 2 + 1) * bs] = total

    sides = ((0, 1), (1, 3))
    dz_order = (2, 1, 3, 0)

    def aggregate_start(feat, terms, hop, ssem, rhsem):
        def one(dy):
            y2 = lax.rem(y + dy, NY)
            total = dot(dense[0, y2], feat[0].reshape(nq * bs, -1))
            total = total + dot(dense[1, y2], feat[1].reshape(nq * bs, -1))
            terms[y2] = total.astype(BF16).reshape(terms.shape[1:])

        one(2)
        for k, dz in enumerate(dz_order):
            for side, dy in sides:
                part = terms.at[ys(2), zs(dz), pl.ds(side * half, half)]
                send(part, hop.at[k, side], ssem.at[NZ], rhsem.at[k], dev(y2=ys(dy)))
        loop(0, 3, lambda i: one(1 + 2 * i - i // 2))

    def aggregate_on(k, terms, hop, ybuf, ssem, rhsem, rysem):
        z2 = zs(dz_order[k])
        wait(hop.at[k], rhsem.at[k])
        if k >= AHEAD:
            wait(ybuf.at[k - AHEAD], ssem.at[k - AHEAD])
        for side, dy in sides:
            y2 = ys(dy)
            at = pl.ds(side * half, half)
            both = terms[y2, z2, at].astype(F32) + hop[k, side].astype(F32)
            terms[y2, z2, at] = both.astype(BF16)
            send(terms.at[y2, z2], ybuf.at[k, side], ssem.at[k], rysem.at[k], dev(y2=y2))

    def aggregate_fold(k, terms, ybuf, zsend, zrecv, ssem, rysem, rzsem):
        dz = dz_order[k]
        wait(ybuf.at[k], rysem.at[k])
        total = terms[y, zs(dz)].astype(F32) + ybuf[k, 0].astype(F32) + ybuf[k, 1].astype(F32)
        if dz:
            zsend[k] = total.astype(BF16)
            send(zsend.at[k], zrecv.at[k], ssem.at[NZ + 1], rzsem.at[0], dev(z2=zs(dz)))
        else:
            own_sum[...] = total

    def aggregate_end(zrecv, rzsem):
        wait(zrecv, rzsem.at[0])
        total = own_sum[...]
        for k in range(NZ - 1):
            total = total + zrecv[k].astype(F32)
        return total.astype(BF16)

    def aggregate_sent(hop, ybuf, zsend, ssem):
        wait(hop, ssem.at[NZ])
        wait(zsend, ssem.at[NZ + 1])
        for k in range(NZ - AHEAD, NZ):
            wait(ybuf.at[k], ssem.at[k])

    def on1(k):
        aggregate_on(k, terms1, hop1, ybuf1, s_rs1, rh_rs1, ry_rs1)

    def on2(k):
        aggregate_on(k, terms2, hop2, ybuf2, s_rs2, rh_rs2, ry_rs2)

    def fold1(k):
        aggregate_fold(k, terms1, ybuf1, zsend1, zrecv1, s_rs1, ry_rs1, rz_rs1)

    def fold2(k):
        aggregate_fold(k, terms2, ybuf2, zsend2, zrecv2, s_rs2, ry_rs2, rz_rs2)

    two = 2 * bs

    def transposed_terms(par, n):
        col = pl.ds(pl.multiple_of(n * two, two), two)
        total = None
        for y2 in range(NY):
            left = jnp.concatenate([cotb[z2, y2] for z2 in range(NZ)], axis=1)
            part = dot(left, dense[par, y2, :, col])
            total = part if total is None else total + part
        return total

    def t_other(n):
        total = transposed_terms(1 - core, n).astype(BF16)
        tsend[2 * n] = total[:, :bs]
        tsend[2 * n + 1] = total[:, bs:]
        pair = pl.ds(2 * n, 2)
        send(tsend.at[pair], trecv.at[pair], s_t.at[0], rs_t.at[n], sib)

    def t_own(n):
        total = transposed_terms(core, n)
        wait(trecv.at[pl.ds(2 * n, 2)], rs_t.at[n])
        town[2 * n] = (total[:, :bs] + trecv[2 * n].astype(F32)).astype(BF16)
        town[2 * n + 1] = (total[:, bs:] + trecv[2 * n + 1].astype(F32)).astype(BF16)

    def t_chips():
        def one(d):
            q2 = chip_at(d)
            send(town.at[q2], tchip.at[d - 1], s_t.at[1], rc_t.at[0], (2 * q2 + core, c))

        loop(1, nq, one)

    def t_sent():
        wait(tsend, s_t.at[0])
        wait(tchip, s_t.at[1])

    def first_layer():
        mixed = aggregate_end(zrecv1, rz_rs1)
        mixed_s[...] = mixed
        pre = dot(mixed, w1_ref[...])
        pre_s[...] = pre
        hidden = (pre / (1.0 + jnp.exp(-pre))).astype(BF16)
        hidden_s[...] = hidden
        second[...] = dot(hidden, w2_ref[...]).astype(BF16)
        gather_start(second, feat2, s_ag2, r_ag2, f_ag2)
        feat2[core, q] = second[...]

    def gradients():
        wait(tchip, rc_t.at[0])
        up = town[q].astype(F32)
        for d in range(nq - 1):
            up = up + tchip[d].astype(F32)
        up = up.T.astype(BF16)
        second_grad = dot_dims(hidden_s[...], up, 0, 0) * scale
        glocal[1] = jnp.concatenate([second_grad[:width], second_grad[width:]], axis=1).astype(BF16)
        back = dot_dims(up, w2_ref[...], 1, 1)
        pre = pre_s[...]
        gate = 1.0 / (1.0 + jnp.exp(-pre))
        back_pre = (back * gate * (1.0 + pre * (1.0 - gate))).astype(BF16)
        glocal[0] = (dot_dims(mixed_s[...], back_pre, 0, 0) * scale).astype(BF16)
        send(glocal.at[1 - core], gsib, s_g.at[0], rs_g.at[0], sib)

    share = gplane.shape[1]
    place = x * NY + y

    def in_plane(d):
        m = lax.rem(place + d, NX * NY)
        return m, dev(x2=m // NY, y2=lax.rem(m, NY))

    def g_plane():
        wait(gsib, rs_g.at[0])
        both = glocal[core].astype(F32) + gsib[...].astype(F32)
        gplane[...] = both.astype(BF16).reshape(gplane.shape)

        def one(d):
            m, device = in_plane(d)
            send(gplane.at[m], gplane_r.at[d - 1], s_g.at[1], rp_g.at[0], device)

        loop(1, NX * NY, one)

    line = z * NL + l

    def g_line():
        wait(gplane_r, rp_g.at[0])
        total = gplane[place].astype(F32)
        for d in range(NX * NY - 1):
            total = total + gplane_r[d].astype(F32)
        gline[line] = total.astype(BF16)
        own = gline.at[line]

        def one(d):
            there = lax.rem(line + d, NZ * NL)
            send(own, own, s_g.at[2], rl_g.at[0], dev(l2=lax.rem(there, NL), z2=there // NL))

        loop(1, NZ * NL, one)

    def g_gather():
        wait(gline.at[pl.ds(0, NZ * NL - 1)], rl_g.at[0])
        total = gline[0].astype(F32)
        for i in range(1, NZ * NL):
            total = total + gline[i].astype(F32)
        gfin[core, place] = total.astype(BF16)
        own = gfin.at[core, place]
        loop(1, NX * NY, lambda d: send(own, own, s_g.at[3], ra_g.at[0], in_plane(d)[1]))

    def g_core():
        wait(gplane_r, ra_g.at[0])
        send(gfin.at[core], gfin.at[core], s_g.at[4], rf_g.at[0], sib)
        g_own_out.start()

    def g_out():
        wait(gfin.at[1 - core], rf_g.at[0])
        g_sib_out.start()
        g_own_out.wait()
        g_sib_out.wait()

    def g_sent():
        wait(gsib, s_g.at[0])
        wait(gplane_r, s_g.at[1])
        wait(gline.at[pl.ds(0, NZ * NL - 1)], s_g.at[2])
        wait(gplane_r, s_g.at[3])
        wait(gfin.at[0], s_g.at[4])

    cot_turn()
    greeted(barrier)
    greet(near2)
    gather_start(x_hbm, feat1, s_ag1, r_ag1, f_ag1)
    cot_z(1)
    cot_z(3)
    cot_y(0)
    fetch[2].wait()
    loop(0, rep // 2, densify)
    greeted(near2)
    greet(near3)
    cot_z(2)
    gather_pass(feat1, s_ag1, r_ag1, f_ag1, [0])
    cot_y(1)
    cot_y(3)
    gather_pass(feat1, s_ag1, r_ag1, f_ag1, [1])
    loop(rep // 2, rep, densify)
    gather_pass(feat1, s_ag1, r_ag1, f_ag1, range(2, 7))
    cot_on(0)
    cot_y(2)
    fetch[1].wait()
    gather_end(feat1, f_ag1)
    aggregate_start(feat1, terms1, hop1, s_rs1, rh_rs1)
    cot_on(1)
    cot_on(3)
    on1(0)
    on1(1)
    on1(2)
    on1(3)
    cot_on(2)
    fold1(0)
    fold1(1)
    fold1(2)
    fold1(3)
    cot_end()
    loop(0, nq // 2, t_other)
    loop(0, nq // 2, t_own)
    t_chips()
    greeted(near3)
    fetch[3].wait()
    fetch[4].wait()
    first_layer()
    gradients()
    gather_pass(feat2, s_ag2, r_ag2, f_ag2, [0, 1])
    g_plane()
    gather_pass(feat2, s_ag2, r_ag2, f_ag2, [2, 3, 4, 5, 6])
    gather_end(feat2, f_ag2)
    aggregate_start(feat2, terms2, hop2, s_rs2, rh_rs2)
    g_line()
    on2(0)
    on2(1)
    on2(2)
    on2(3)
    fold2(0)
    g_gather()
    fold2(1)
    fold2(2)
    fold2(3)
    g_core()
    emb_s[...] = aggregate_end(zrecv2, rz_rs2)
    emb_out.start()
    g_out()
    emb_out.wait()

    gather_sent(feat1, s_ag1)
    cot_sent()
    aggregate_sent(hop1, ybuf1, zsend1, s_rs1)
    gather_sent(feat2, s_ag2)
    aggregate_sent(hop2, ybuf2, zsend2, s_rs2)
    t_sent()
    g_sent()


def finish(emb_in, g_in, emb_out, g1_out, g2_out, g_s, g1_s, g2_s, sems):
    width = g1_s.shape[0]
    emb = pltpu.make_async_copy(emb_in, emb_out, sems.at[0])
    first_in = pltpu.make_async_copy(g_in.at[0], g_s.at[0], sems.at[1])
    second_in = pltpu.make_async_copy(g_in.at[1], g_s.at[1], sems.at[2])
    first_out = pltpu.make_async_copy(g1_s, g1_out, sems.at[3])
    second_out = pltpu.make_async_copy(g2_s, g2_out, sems.at[4])
    first_in.start()
    second_in.start()
    emb.start()
    first_in.wait()
    g1_s[...] = g_s[0].reshape(g1_s.shape).astype(F32)
    first_out.start()
    second_in.wait()
    grad = g_s[1].reshape(g1_s.shape).astype(F32)
    g2_s[:width] = grad[:, :width]
    g2_s[width:] = grad[:, width:]
    second_out.start()
    emb.wait()
    first_out.wait()
    second_out.wait()


def shards(nodes, node_features, adjacency, column_ids, block_counts, w1, w2, cotangent):
    rep, nq = NY * NZ, NL * NX
    bs, width = node_features.shape
    hid = w1.shape[1]
    block = (bs, width)
    turned = (width, bs)
    share = (width // (NX * NY), hid)
    vmem = pl.BlockSpec(memory_space=pltpu.VMEM)
    smem = pl.BlockSpec(memory_space=pltpu.SMEM)
    hbm = pl.BlockSpec(memory_space=pl.ANY)
    v = pltpu.VMEM
    dma = pltpu.SemaphoreType.DMA
    scratch = [
        v(adjacency.shape, BF16),
        v(w1.shape, BF16),
        v(w2.shape, BF16),
        v(block, BF16),
        v((2, NY, NZ * bs, nq * bs), BF16),
        v((2, nq) + block, BF16),
        v((2, nq) + block, BF16),
        v((NZ, NY) + turned, BF16),
        v((NY, NZ) + block, BF16),
        v((NY, NZ) + block, BF16),
        v((NZ, 2, bs // 2, width), BF16),
        v((NZ, 2, bs // 2, width), BF16),
        v((NZ, 2) + block, BF16),
        v((NZ, 2) + block, BF16),
        v((NZ - 1,) + block, BF16),
        v((NZ - 1,) + block, BF16),
        v((NZ - 1,) + block, BF16),
        v((NZ - 1,) + block, BF16),
        v(block, F32),
        v(block, BF16),
        v(block, BF16),
        v((nq,) + turned, BF16),
        v((nq,) + turned, BF16),
        v((nq,) + turned, BF16),
        v((nq - 1,) + turned, BF16),
        v(block, BF16),
        v((bs, hid), BF16),
        v((bs, hid), F32),
        v((2, width, hid), BF16),
        v((width, hid), BF16),
        v((NX * NY,) + share, BF16),
        v((NX * NY - 1,) + share, BF16),
        v((NZ * NL,) + share, BF16),
        v((2, NX * NY) + share, BF16),
        pltpu.SemaphoreType.REGULAR,
        pltpu.SemaphoreType.REGULAR,
    ]
    ag = [dma((2,)), dma((7,)), dma((1,))]
    rs = [dma((NZ + 2,)), dma((NZ,)), dma((NZ,)), dma((1,))]
    scratch += ag + ag
    scratch += [dma((2,)), dma((NZ - 1,)), dma((NZ, 3))]
    scratch += rs + rs
    scratch += [dma((2,)), dma((nq // 2,)), dma((1,))]
    scratch += [dma((5,)), dma((1,)), dma((1,)), dma((1,)), dma((1,)), dma((1,)), dma((5,)), dma((3,))]
    embedding, grads = pl.pallas_call(
        functools.partial(kernel, 1.0 / math.sqrt(nodes)),
        out_shape=(
            jax.ShapeDtypeStruct(block, BF16),
            jax.ShapeDtypeStruct((2, NX * NY) + share, BF16),
        ),
        in_specs=[smem, smem, hbm, hbm, hbm, hbm, hbm],
        out_specs=(hbm, hbm),
        scratch_shapes=scratch,
        compiler_params=pltpu.CompilerParams(
            collective_id=0, has_side_effects=True, vmem_limit_bytes=VMEM_BYTES
        ),
        name="graph_step",
    )(column_ids.T, block_counts.T, node_features, adjacency, w1, w2, cotangent)
    return pl.pallas_call(
        finish,
        out_shape=(
            jax.ShapeDtypeStruct(block, BF16),
            jax.ShapeDtypeStruct((width, hid), F32),
            jax.ShapeDtypeStruct((hid, width), F32),
        ),
        in_specs=[hbm, hbm],
        out_specs=(hbm, hbm, hbm),
        scratch_shapes=[
            v(grads.shape, BF16),
            v((width, hid), F32),
            v((hid, width), F32),
            dma((5,)),
        ],
        compiler_params=pltpu.CompilerParams(vmem_limit_bytes=VMEM_BYTES),
        name="finish",
    )(embedding, grads)


def solution(mesh):
    in_specs = (
        P(("rows", "rep"), None),
        P("rows", "rep", None, None),
        P("rows", "rep"),
        P("rows", "rep"),
        P(),
        P(),
        P(("rows", "rep"), None),
    )
    out_specs = (P(("rows", "rep"), None), P(), P())

    def run(node_features, *rest):
        body = functools.partial(shards, node_features.shape[0])
        return jax.shard_map(
            body, mesh=mesh, in_specs=in_specs, out_specs=out_specs, check_vma=False
        )(node_features, *rest)

    return run
```

```python
import functools
import math

import jax
import jax.numpy as jnp
from jax import lax
from jax.experimental import pallas as pl
from jax.experimental.pallas import tpu as pltpu
from jax.sharding import PartitionSpec as P

MESH = pl.DeviceIdType.MESH
F32 = jnp.float32
BF16 = jnp.bfloat16
VMEM_BYTES = 63 * 1024 * 1024
NL, NX, NY, NZ = 2, 4, 4, 4
AHEAD = 4
TAIL = 16


def dot(a, b):
    return jnp.dot(a, b, preferred_element_type=F32)


def dot_dims(a, b, ca, cb):
    return lax.dot_general(a, b, (((ca,), (cb,)), ((), ())), preferred_element_type=F32)


def loop(lo, hi, body):
    def step(i, carry):
        body(i)
        return carry

    lax.fori_loop(lo, hi, step, 0)


def kernel(
    scale,
    ids,
    counts,
    x_hbm,
    adj_hbm,
    w1_hbm,
    w2_hbm,
    cot_hbm,
    emb_hbm,
    g_hbm,
    adj_ref,
    w1_ref,
    w2_ref,
    cot_ref,
    dense,
    feat1,
    feat2,
    cotb,
    terms1,
    terms2,
    hop1,
    zfirst,
    ztail,
    ytail,
    ybuf1,
    ybuf2,
    zsend1,
    zsend2,
    zrecv1,
    zrecv2,
    own_sum,
    second,
    emb_s,
    tnear,
    tsend,
    trecv,
    town,
    tchip,
    mixed_s,
    hidden_s,
    pre_s,
    glocal,
    gsib,
    gplane,
    gplane_r,
    gline,
    gfin,
    near2,
    near3,
    s_ag1,
    r_ag1,
    f_ag1,
    s_ag2,
    r_ag2,
    f_ag2,
    s_cot,
    rz_cot,
    ry_cot,
    s_rs1,
    rh_rs1,
    ry_rs1,
    rz_rs1,
    s_rs2,
    ry_rs2,
    rz_rs2,
    rf_rs2,
    s_t,
    rs_t,
    rc_t,
    s_g,
    rs_g,
    rp_g,
    rl_g,
    ra_g,
    rf_g,
    s_in,
    s_out,
):
    rows, rep = 2 * NL * NX, NY * NZ
    nq = NL * NX
    bs = x_hbm.shape[0]
    half = bs // 2
    r = lax.axis_index("rows")
    c = lax.axis_index("rep")
    core = lax.rem(r, 2)
    q = r // 2
    l = q // NX
    x = lax.rem(q, NX)
    y = c // NZ
    z = lax.rem(c, NZ)
    sib = (r + 1 - 2 * core, c)

    def xs(d):
        return lax.rem(x + d, NX)

    def ys(d):
        return lax.rem(y + d, NY)

    def zs(d):
        return lax.rem(z + d, NZ)

    def dev(l2=l, x2=x, y2=y, z2=z):
        return ((l2 * NX + x2) * 2 + core, y2 * NZ + z2)

    def chip_at(d):
        return lax.rem(q + d, nq)

    def send(src, dst, ssem, rsem, device):
        pltpu.make_async_remote_copy(
            src_ref=src, dst_ref=dst, send_sem=ssem, recv_sem=rsem, device_id=device, device_id_type=MESH
        ).start()

    def wait(ref, sem):
        pltpu.make_async_copy(ref, ref, sem).wait()

    near = [
        sib,
        dev(l2=1 - l),
        dev(x2=xs(1)),
        dev(x2=xs(2)),
        dev(x2=xs(3)),
        dev(y2=ys(1)),
        dev(y2=ys(3)),
        dev(z2=zs(1)),
        dev(z2=zs(3)),
    ]

    def greet(sem):
        for device in near:
            pl.semaphore_signal(sem, inc=1, device_id=device, device_id_type=MESH)

    def greeted(sem):
        pl.semaphore_wait(sem, len(near))

    barrier = pltpu.get_barrier_semaphore()
    greet(barrier)
    emb_out = pltpu.make_async_copy(emb_s, emb_hbm, s_out.at[0])
    g_own_out = pltpu.make_async_copy(gfin.at[core], g_hbm.at[core], s_out.at[1])
    g_sib_out = pltpu.make_async_copy(gfin.at[1 - core], g_hbm.at[1 - core], s_out.at[2])
    fetch = [
        pltpu.make_async_copy(src, dst, s_in.at[i])
        for i, (src, dst) in enumerate(
            [
                (cot_hbm, cot_ref),
                (x_hbm, feat1.at[core, q]),
                (adj_hbm, adj_ref),
                (w1_hbm, w1_ref),
                (w2_hbm, w2_ref),
            ]
        )
    ]
    for copy in fetch:
        copy.start()

    def gather_start(src, buf, ssem, rsem, fsem):
        to = buf.at[core, q]
        for i, device in enumerate([dev(l2=1 - l), dev(x2=xs(2)), dev(x2=xs(1)), dev(x2=xs(3))]):
            send(src, to, ssem.at[0], rsem.at[i], device)
        send(src, to, ssem.at[0], fsem.at[0], sib)

    def gather_pass(buf, ssem, rsem, fsem, steps):
        there = 1 - l
        came = [
            (there, x, [(4, dev(x2=xs(1))), (5, dev(x2=xs(3)))]),
            (l, xs(2), [(6, dev(l2=there))]),
            (l, xs(3), []),
            (l, xs(1), []),
            (there, xs(3), []),
            (there, xs(1), []),
            (there, xs(2), []),
        ]
        for i in steps:
            l2, x2, onward = came[i]
            block = buf.at[core, l2 * NX + x2]
            wait(block, rsem.at[i])
            for j, device in onward:
                send(block, block, ssem.at[0], rsem.at[j], device)
            send(block, block, ssem.at[1], fsem.at[0], sib)

    def gather_end(buf, fsem):
        wait(buf.at[1 - core], fsem.at[0])

    def gather_sent(buf, ssem):
        wait(buf.at[0], ssem.at[0])
        wait(buf.at[0, pl.ds(0, nq - 1)], ssem.at[1])

    def cot_turn():
        fetch[0].wait()
        cotb[z, y] = cot_ref[...].astype(F32).T.astype(BF16)

    def cot_z(dz):
        own = cotb.at[z, y]
        send(own, own, s_cot.at[0], rz_cot.at[dz - 1], dev(z2=zs(dz)))

    def cot_y(dz):
        block = cotb.at[zs(NZ - dz), y]
        if dz > 0:
            wait(block, rz_cot.at[dz - 1])
        for side, dy in ((0, 1), (1, 3)):
            send(block, block, s_cot.at[1], ry_cot.at[dz, side], dev(y2=ys(dy)))

    def cot_on(dz):
        for side, dy, rows_of in ((0, 1, pl.ds(0, width // 2)), (1, 3, pl.ds(width // 2, width // 2))):
            block = cotb.at[zs(NZ - dz), ys(4 - dy)]
            wait(block, ry_cot.at[dz, side])
            part = block.at[rows_of]
            send(part, part, s_cot.at[1], ry_cot.at[dz, 2], dev(y2=ys(dy)))

    def cot_end():
        for dz in range(NZ):
            wait(cotb.at[zs(NZ - dz), ys(2)], ry_cot.at[dz, 2])

    def cot_sent():
        wait(cotb.at[0, pl.ds(0, NZ - 1)], s_cot.at[0])
        wait(cotb.at[:, pl.ds(0, 3)], s_cot.at[1])

    width = x_hbm.shape[1]

    def densify(b):
        z2 = lax.rem(b, NZ)
        y2 = b // NZ
        blocks = [adj_ref[b, s] for s in range(adj_ref.shape[1])]
        zero = jnp.zeros_like(blocks[0])
        where_to = [jnp.where(s < counts[0, b], ids[s, b], -1) for s in range(len(blocks))]
        row = pl.ds(pl.multiple_of(z2 * bs, bs), bs)
        for p in range(rows):
            total = jnp.where(where_to[0] == p, blocks[0], zero)
            for s in range(1, len(blocks)):
                total = total + jnp.where(where_to[s] == p, blocks[s], zero)
            dense[p % 2, y2, row, (p // 2) * bs : (p // 2 + 1) * bs] = total

    sides = ((0, 1), (1, 3))
    dz_order = (2, 1, 3, 0)

    def aggregate_start(feat, terms, hop, ssem, rhsem):
        def one(dy):
            y2 = lax.rem(y + dy, NY)
            total = dot(dense[0, y2], feat[0].reshape(nq * bs, -1))
            total = total + dot(dense[1, y2], feat[1].reshape(nq * bs, -1))
            terms[y2] = total.astype(BF16).reshape(terms.shape[1:])

        one(2)
        for k, dz in enumerate(dz_order):
            for side, dy in sides:
                part = terms.at[ys(2), zs(dz), pl.ds(side * half, half)]
                send(part, hop.at[k, side], ssem.at[NZ], rhsem.at[k], dev(y2=ys(dy)))
        loop(0, 3, lambda i: one(1 + 2 * i - i // 2))

    def aggregate_on(k, terms, hop, ybuf, ssem, rhsem, rysem):
        z2 = zs(dz_order[k])
        wait(hop.at[k], rhsem.at[k])
        if k >= AHEAD:
            wait(ybuf.at[k - AHEAD], ssem.at[k - AHEAD])
        for side, dy in sides:
            y2 = ys(dy)
            at = pl.ds(side * half, half)
            both = terms[y2, z2, at].astype(F32) + hop[k, side].astype(F32)
            terms[y2, z2, at] = both.astype(BF16)
            send(terms.at[y2, z2], ybuf.at[k, side], ssem.at[k], rysem.at[k], dev(y2=y2))

    def aggregate_fold(k, terms, ybuf, zsend, zrecv, ssem, rysem, rzsem):
        dz = dz_order[k]
        wait(ybuf.at[k], rysem.at[k])
        total = terms[y, zs(dz)].astype(F32) + ybuf[k, 0].astype(F32) + ybuf[k, 1].astype(F32)
        if dz:
            zsend[k] = total.astype(BF16)
            send(zsend.at[k], zrecv.at[k], ssem.at[NZ + 1], rzsem.at[0], dev(z2=zs(dz)))
        else:
            own_sum[...] = total

    def aggregate_end(zrecv, rzsem):
        wait(zrecv, rzsem.at[0])
        total = own_sum[...]
        for k in range(NZ - 1):
            total = total + zrecv[k].astype(F32)
        return total.astype(BF16)

    def aggregate_sent(hop, ybuf, zsend, ssem):
        wait(hop, ssem.at[NZ])
        wait(zsend, ssem.at[NZ + 1])
        for k in range(NZ - AHEAD, NZ):
            wait(ybuf.at[k], ssem.at[k])

    def on1(k):
        aggregate_on(k, terms1, hop1, ybuf1, s_rs1, rh_rs1, ry_rs1)

    def fold1(k):
        aggregate_fold(k, terms1, ybuf1, zsend1, zrecv1, s_rs1, ry_rs1, rz_rs1)

    upper = bs - TAIL

    def second_start():
        def one(k, dz, away):
            z2 = zs(dz)
            row = pl.ds(pl.multiple_of(z2 * bs, bs), bs)
            total = None
            for par in range(2):
                left = jnp.concatenate([dense[par, y2, row] for y2 in range(NY)], axis=0)
                part = dot(left, feat2[par].reshape(nq * bs, -1))
                total = part if total is None else total + part
            terms2[z2] = total.astype(BF16).reshape(terms2.shape[1:])
            if away:
                part = terms2.at[z2, :, pl.ds(upper, TAIL)]
                send(part, zfirst.at[dz - 1], s_rs2.at[2], rf_rs2.at[0], dev(z2=z2))
            for i, dy in enumerate((2, 1, 3)):
                part = terms2.at[z2, ys(dy), pl.ds(0, upper)]
                send(part, ybuf2.at[k, i], s_rs2.at[0], ry_rs2.at[k], dev(y2=ys(dy)))

        loop(0, NZ - 1, lambda k: one(k, 2 - k + 3 * (k // 2), True))
        one(NZ - 1, 0, False)

    def second_tail():
        wait(zfirst, rf_rs2.at[0])
        total = terms2[z, :, upper:].astype(F32)
        for i in range(NZ - 1):
            total = total + zfirst[i].astype(F32)
        ztail[...] = total.astype(BF16)
        for i, dy in enumerate((2, 1, 3)):
            send(ztail.at[ys(dy)], ytail.at[i], s_rs2.at[3], rf_rs2.at[1], dev(y2=ys(dy)))

    def second_fold(k):
        dz = dz_order[k]
        wait(ybuf2.at[k], ry_rs2.at[k])
        total = terms2[zs(dz), y, :upper].astype(F32)
        for i in range(NY - 1):
            total = total + ybuf2[k, i].astype(F32)
        if dz:
            zsend2[k] = total.astype(BF16)
            send(zsend2.at[k], zrecv2.at[k], s_rs2.at[1], rz_rs2.at[0], dev(z2=zs(dz)))
        else:
            own_sum[:upper] = total

    def second_end():
        wait(ytail, rf_rs2.at[1])
        low = ztail[y].astype(F32)
        for i in range(NY - 1):
            low = low + ytail[i].astype(F32)
        wait(zrecv2, rz_rs2.at[0])
        total = own_sum[:upper]
        for k in range(NZ - 1):
            total = total + zrecv2[k].astype(F32)
        emb_s[:upper] = total.astype(BF16)
        emb_s[upper:] = low.astype(BF16)

    def second_sent():
        wait(ybuf2, s_rs2.at[0])
        wait(zsend2, s_rs2.at[1])
        wait(zfirst, s_rs2.at[2])
        wait(ytail, s_rs2.at[3])

    two = 2 * bs

    def transposed_part(par, n, y2):
        col = pl.ds(pl.multiple_of(n * two, two), two)
        left = jnp.concatenate([cotb[z2, y2] for z2 in range(NZ)], axis=1)
        return dot(left, dense[par, y2, :, col])

    def t_near(i):
        par, n = i // (nq // 2), lax.rem(i, nq // 2)
        total = transposed_part(par, n, y) + transposed_part(par, n, ys(1))
        tnear[par, n] = total + transposed_part(par, n, ys(3))

    def t_other(n):
        total = (tnear[1 - core, n] + transposed_part(1 - core, n, ys(2))).astype(BF16)
        tsend[2 * n] = total[:, :bs]
        tsend[2 * n + 1] = total[:, bs:]
        pair = pl.ds(2 * n, 2)
        send(tsend.at[pair], trecv.at[pair], s_t.at[0], rs_t.at[n], sib)

    def t_own(n):
        total = tnear[core, n] + transposed_part(core, n, ys(2))
        wait(trecv.at[pl.ds(2 * n, 2)], rs_t.at[n])
        town[2 * n] = (total[:, :bs] + trecv[2 * n].astype(F32)).astype(BF16)
        town[2 * n + 1] = (total[:, bs:] + trecv[2 * n + 1].astype(F32)).astype(BF16)

    def t_chips():
        def one(d):
            q2 = chip_at(d)
            send(town.at[q2], tchip.at[d - 1], s_t.at[1], rc_t.at[0], (2 * q2 + core, c))

        loop(1, nq, one)

    def t_sent():
        wait(tsend, s_t.at[0])
        wait(tchip, s_t.at[1])

    def first_layer():
        mixed = aggregate_end(zrecv1, rz_rs1)
        mixed_s[...] = mixed
        pre = dot(mixed, w1_ref[...])
        pre_s[...] = pre
        hidden = (pre / (1.0 + jnp.exp(-pre))).astype(BF16)
        hidden_s[...] = hidden
        second[...] = dot(hidden, w2_ref[...]).astype(BF16)
        gather_start(second, feat2, s_ag2, r_ag2, f_ag2)
        feat2[core, q] = second[...]

    def gradients():
        wait(tchip, rc_t.at[0])
        up = town[q].astype(F32)
        for d in range(nq - 1):
            up = up + tchip[d].astype(F32)
        up = up.T.astype(BF16)
        second_grad = dot_dims(hidden_s[...], up, 0, 0) * scale
        glocal[1] = jnp.concatenate([second_grad[:width], second_grad[width:]], axis=1).astype(BF16)
        back = dot_dims(up, w2_ref[...], 1, 1)
        pre = pre_s[...]
        gate = 1.0 / (1.0 + jnp.exp(-pre))
        back_pre = (back * gate * (1.0 + pre * (1.0 - gate))).astype(BF16)
        glocal[0] = (dot_dims(mixed_s[...], back_pre, 0, 0) * scale).astype(BF16)
        send(glocal.at[1 - core], gsib, s_g.at[0], rs_g.at[0], sib)

    share = gplane.shape[1]
    place = x * NY + y

    def in_plane(d):
        m = lax.rem(place + d, NX * NY)
        return m, dev(x2=m // NY, y2=lax.rem(m, NY))

    def g_plane():
        wait(gsib, rs_g.at[0])
        both = glocal[core].astype(F32) + gsib[...].astype(F32)
        gplane[...] = both.astype(BF16).reshape(gplane.shape)

        def one(d):
            m, device = in_plane(d)
            send(gplane.at[m], gplane_r.at[d - 1], s_g.at[1], rp_g.at[0], device)

        loop(1, NX * NY, one)

    line = z * NL + l

    def g_line():
        wait(gplane_r, rp_g.at[0])
        total = gplane[place].astype(F32)
        for d in range(NX * NY - 1):
            total = total + gplane_r[d].astype(F32)
        gline[line] = total.astype(BF16)
        own = gline.at[line]

        def one(d):
            there = lax.rem(line + d, NZ * NL)
            send(own, own, s_g.at[2], rl_g.at[0], dev(l2=lax.rem(there, NL), z2=there // NL))

        loop(1, NZ * NL, one)

    def g_gather():
        wait(gline.at[pl.ds(0, NZ * NL - 1)], rl_g.at[0])
        total = gline[0].astype(F32)
        for i in range(1, NZ * NL):
            total = total + gline[i].astype(F32)
        gfin[core, place] = total.astype(BF16)
        own = gfin.at[core, place]
        loop(1, NX * NY, lambda d: send(own, own, s_g.at[3], ra_g.at[0], in_plane(d)[1]))

    def g_core():
        wait(gplane_r, ra_g.at[0])
        send(gfin.at[core], gfin.at[core], s_g.at[4], rf_g.at[0], sib)
        g_own_out.start()

    def g_out():
        wait(gfin.at[1 - core], rf_g.at[0])
        g_sib_out.start()
        g_own_out.wait()
        g_sib_out.wait()

    def g_sent():
        wait(gsib, s_g.at[0])
        wait(gplane_r, s_g.at[1])
        wait(gline.at[pl.ds(0, NZ * NL - 1)], s_g.at[2])
        wait(gplane_r, s_g.at[3])
        wait(gfin.at[0], s_g.at[4])

    cot_turn()
    greeted(barrier)
    greet(near2)
    gather_start(x_hbm, feat1, s_ag1, r_ag1, f_ag1)
    cot_z(1)
    cot_z(3)
    cot_y(0)
    fetch[2].wait()
    loop(0, rep // 2, densify)
    greeted(near2)
    greet(near3)
    cot_z(2)
    gather_pass(feat1, s_ag1, r_ag1, f_ag1, [0])
    cot_y(1)
    cot_y(3)
    gather_pass(feat1, s_ag1, r_ag1, f_ag1, [1])
    loop(rep // 2, rep, densify)
    gather_pass(feat1, s_ag1, r_ag1, f_ag1, range(2, 7))
    cot_on(0)
    cot_y(2)
    fetch[1].wait()
    gather_end(feat1, f_ag1)
    aggregate_start(feat1, terms1, hop1, s_rs1, rh_rs1)
    cot_on(1)
    cot_on(3)
    on1(0)
    on1(1)
    on1(2)
    on1(3)
    cot_on(2)
    loop(0, nq, t_near)
    fold1(0)
    fold1(1)
    cot_end()
    loop(0, nq // 2, t_other)
    fold1(2)
    loop(0, nq // 2, t_own)
    t_chips()
    fold1(3)
    greeted(near3)
    fetch[3].wait()
    fetch[4].wait()
    first_layer()
    gather_pass(feat2, s_ag2, r_ag2, f_ag2, [0])
    gradients()
    gather_pass(feat2, s_ag2, r_ag2, f_ag2, [1])
    g_plane()
    gather_pass(feat2, s_ag2, r_ag2, f_ag2, [2, 3, 4, 5, 6])
    gather_end(feat2, f_ag2)
    second_start()
    g_line()
    second_fold(0)
    second_fold(1)
    second_tail()
    g_gather()
    second_fold(2)
    second_fold(3)
    g_core()
    second_end()
    emb_out.start()
    g_out()
    emb_out.wait()

    gather_sent(feat1, s_ag1)
    cot_sent()
    aggregate_sent(hop1, ybuf1, zsend1, s_rs1)
    gather_sent(feat2, s_ag2)
    second_sent()
    t_sent()
    g_sent()


def finish(emb_in, g_in, emb_out, g1_out, g2_out, g_s, g1_s, g2_s, sems):
    width = g1_s.shape[0]
    emb = pltpu.make_async_copy(emb_in, emb_out, sems.at[0])
    first_in = pltpu.make_async_copy(g_in.at[0], g_s.at[0], sems.at[1])
    second_in = pltpu.make_async_copy(g_in.at[1], g_s.at[1], sems.at[2])
    first_out = pltpu.make_async_copy(g1_s, g1_out, sems.at[3])
    second_out = pltpu.make_async_copy(g2_s, g2_out, sems.at[4])
    first_in.start()
    second_in.start()
    emb.start()
    first_in.wait()
    g1_s[...] = g_s[0].reshape(g1_s.shape).astype(F32)
    first_out.start()
    second_in.wait()
    grad = g_s[1].reshape(g1_s.shape).astype(F32)
    g2_s[:width] = grad[:, :width]
    g2_s[width:] = grad[:, width:]
    second_out.start()
    emb.wait()
    first_out.wait()
    second_out.wait()


def shards(nodes, node_features, adjacency, column_ids, block_counts, w1, w2, cotangent):
    rep, nq = NY * NZ, NL * NX
    bs, width = node_features.shape
    hid = w1.shape[1]
    block = (bs, width)
    turned = (width, bs)
    upper = (bs - TAIL, width)
    share = (width // (NX * NY), hid)
    vmem = pl.BlockSpec(memory_space=pltpu.VMEM)
    smem = pl.BlockSpec(memory_space=pltpu.SMEM)
    hbm = pl.BlockSpec(memory_space=pl.ANY)
    v = pltpu.VMEM
    dma = pltpu.SemaphoreType.DMA
    scratch = [
        v(adjacency.shape, BF16),
        v(w1.shape, BF16),
        v(w2.shape, BF16),
        v(block, BF16),
        v((2, NY, NZ * bs, nq * bs), BF16),
        v((2, nq) + block, BF16),
        v((2, nq) + block, BF16),
        v((NZ, NY) + turned, BF16),
        v((NY, NZ) + block, BF16),
        v((NY, NZ) + block, BF16),
        v((NZ, 2, bs // 2, width), BF16),
        v((NZ - 1, NY, TAIL, width), BF16),
        v((NY, TAIL, width), BF16),
        v((NY - 1, TAIL, width), BF16),
        v((NZ, 2) + block, BF16),
        v((NZ, NY - 1) + upper, BF16),
        v((NZ - 1,) + block, BF16),
        v((NZ - 1,) + upper, BF16),
        v((NZ - 1,) + block, BF16),
        v((NZ - 1,) + upper, BF16),
        v(block, F32),
        v(block, BF16),
        v(block, BF16),
        v((2, nq // 2, width, 2 * bs), F32),
        v((nq,) + turned, BF16),
        v((nq,) + turned, BF16),
        v((nq,) + turned, BF16),
        v((nq - 1,) + turned, BF16),
        v(block, BF16),
        v((bs, hid), BF16),
        v((bs, hid), F32),
        v((2, width, hid), BF16),
        v((width, hid), BF16),
        v((NX * NY,) + share, BF16),
        v((NX * NY - 1,) + share, BF16),
        v((NZ * NL,) + share, BF16),
        v((2, NX * NY) + share, BF16),
        pltpu.SemaphoreType.REGULAR,
        pltpu.SemaphoreType.REGULAR,
    ]
    ag = [dma((2,)), dma((7,)), dma((1,))]
    rs = [dma((NZ + 2,)), dma((NZ,)), dma((NZ,)), dma((1,))]
    scratch += ag + ag
    scratch += [dma((2,)), dma((NZ - 1,)), dma((NZ, 3))]
    scratch += rs + [dma((4,)), dma((NZ,)), dma((1,)), dma((2,))]
    scratch += [dma((2,)), dma((nq // 2,)), dma((1,))]
    scratch += [dma((5,)), dma((1,)), dma((1,)), dma((1,)), dma((1,)), dma((1,)), dma((5,)), dma((3,))]
    embedding, grads = pl.pallas_call(
        functools.partial(kernel, 1.0 / math.sqrt(nodes)),
        out_shape=(
            jax.ShapeDtypeStruct(block, BF16),
            jax.ShapeDtypeStruct((2, NX * NY) + share, BF16),
        ),
        in_specs=[smem, smem, hbm, hbm, hbm, hbm, hbm],
        out_specs=(hbm, hbm),
        scratch_shapes=scratch,
        compiler_params=pltpu.CompilerParams(
            collective_id=0, has_side_effects=True, vmem_limit_bytes=VMEM_BYTES
        ),
        name="graph_step",
    )(column_ids.T, block_counts.T, node_features, adjacency, w1, w2, cotangent)
    return pl.pallas_call(
        finish,
        out_shape=(
            jax.ShapeDtypeStruct(block, BF16),
            jax.ShapeDtypeStruct((width, hid), F32),
            jax.ShapeDtypeStruct((hid, width), F32),
        ),
        in_specs=[hbm, hbm],
        out_specs=(hbm, hbm, hbm),
        scratch_shapes=[
            v(grads.shape, BF16),
            v((width, hid), F32),
            v((hid, width), F32),
            dma((5,)),
        ],
        compiler_params=pltpu.CompilerParams(vmem_limit_bytes=VMEM_BYTES),
        name="finish",
    )(embedding, grads)


def solution(mesh):
    in_specs = (
        P(("rows", "rep"), None),
        P("rows", "rep", None, None),
        P("rows", "rep"),
        P("rows", "rep"),
        P(),
        P(),
        P(("rows", "rep"), None),
    )
    out_specs = (P(("rows", "rep"), None), P(), P())

    def run(node_features, *rest):
        body = functools.partial(shards, node_features.shape[0])
        return jax.shard_map(
            body, mesh=mesh, in_specs=in_specs, out_specs=out_specs, check_vma=False
        )(node_features, *rest)

    return run
```

```python
import functools
import math

import jax
import jax.numpy as jnp
from jax import lax
from jax.experimental import pallas as pl
from jax.experimental.pallas import tpu as pltpu
from jax.sharding import PartitionSpec as P

MESH = pl.DeviceIdType.MESH
F32 = jnp.float32
BF16 = jnp.bfloat16
VMEM_BYTES = 63 * 1024 * 1024
NL, NX, NY, NZ = 2, 4, 4, 4
AHEAD = 4
TAIL = 16


def dot(a, b):
    return jnp.dot(a, b, preferred_element_type=F32)


def dot_dims(a, b, ca, cb):
    return lax.dot_general(a, b, (((ca,), (cb,)), ((), ())), preferred_element_type=F32)


def loop(lo, hi, body):
    def step(i, carry):
        body(i)
        return carry

    lax.fori_loop(lo, hi, step, 0)


def kernel(
    scale,
    ids,
    counts,
    x_hbm,
    adj_hbm,
    w1_hbm,
    w2_hbm,
    cot_hbm,
    emb_hbm,
    g_hbm,
    adj_ref,
    w1_ref,
    w2_ref,
    cot_ref,
    dense,
    feat1,
    feat2,
    cotb,
    terms1,
    terms2,
    hop1,
    zfirst,
    ztail,
    ytail,
    ybuf1,
    ybuf2,
    zsend1,
    zsend2,
    zrecv1,
    zrecv2,
    own_sum,
    second,
    emb_s,
    tnear,
    tsend,
    trecv,
    town,
    tchip,
    mixed_s,
    hidden_s,
    pre_s,
    glocal,
    gsib,
    gplane,
    gplane_r,
    gline,
    gfin,
    near2,
    near3,
    s_ag1,
    r_ag1,
    f_ag1,
    s_ag2,
    r_ag2,
    f_ag2,
    s_cot,
    rz_cot,
    ry_cot,
    s_rs1,
    rh_rs1,
    ry_rs1,
    rz_rs1,
    s_rs2,
    ry_rs2,
    rz_rs2,
    rf_rs2,
    s_t,
    rs_t,
    rc_t,
    s_g,
    rs_g,
    rp_g,
    rl_g,
    ra_g,
    rf_g,
    s_in,
    s_out,
):
    rows, rep = 2 * NL * NX, NY * NZ
    nq = NL * NX
    bs = x_hbm.shape[0]
    half = bs // 2
    r = lax.axis_index("rows")
    c = lax.axis_index("rep")
    core = lax.rem(r, 2)
    q = r // 2
    l = q // NX
    x = lax.rem(q, NX)
    y = c // NZ
    z = lax.rem(c, NZ)
    sib = (r + 1 - 2 * core, c)

    def xs(d):
        return lax.rem(x + d, NX)

    def ys(d):
        return lax.rem(y + d, NY)

    def zs(d):
        return lax.rem(z + d, NZ)

    def dev(l2=l, x2=x, y2=y, z2=z):
        return ((l2 * NX + x2) * 2 + core, y2 * NZ + z2)

    def chip_at(d):
        return lax.rem(q + d, nq)

    def send(src, dst, ssem, rsem, device):
        pltpu.make_async_remote_copy(
            src_ref=src, dst_ref=dst, send_sem=ssem, recv_sem=rsem, device_id=device, device_id_type=MESH
        ).start()

    def wait(ref, sem):
        pltpu.make_async_copy(ref, ref, sem).wait()

    near = [
        sib,
        dev(l2=1 - l),
        dev(x2=xs(1)),
        dev(x2=xs(2)),
        dev(x2=xs(3)),
        dev(y2=ys(1)),
        dev(y2=ys(3)),
        dev(z2=zs(1)),
        dev(z2=zs(3)),
    ]

    def greet(sem):
        for device in near:
            pl.semaphore_signal(sem, inc=1, device_id=device, device_id_type=MESH)

    def greeted(sem):
        pl.semaphore_wait(sem, len(near))

    barrier = pltpu.get_barrier_semaphore()
    greet(barrier)
    emb_out = pltpu.make_async_copy(emb_s, emb_hbm, s_out.at[0])
    g_own_out = pltpu.make_async_copy(gfin.at[core], g_hbm.at[core], s_out.at[1])
    fetch = [
        pltpu.make_async_copy(src, dst, s_in.at[i])
        for i, (src, dst) in enumerate(
            [
                (cot_hbm, cot_ref),
                (x_hbm, feat1.at[core, q]),
                (adj_hbm, adj_ref),
                (w1_hbm, w1_ref),
                (w2_hbm, w2_ref),
            ]
        )
    ]
    for copy in fetch:
        copy.start()

    def gather_start(src, buf, ssem, rsem, fsem):
        to = buf.at[core, q]
        for i, device in enumerate([dev(l2=1 - l), dev(x2=xs(2)), dev(x2=xs(1)), dev(x2=xs(3))]):
            send(src, to, ssem.at[0], rsem.at[i], device)
        send(src, to, ssem.at[0], fsem.at[0], sib)

    def gather_pass(buf, ssem, rsem, fsem, steps):
        there = 1 - l
        came = [
            (there, x, [(4, dev(x2=xs(1))), (5, dev(x2=xs(3)))]),
            (l, xs(2), [(6, dev(l2=there))]),
            (l, xs(3), []),
            (l, xs(1), []),
            (there, xs(3), []),
            (there, xs(1), []),
            (there, xs(2), []),
        ]
        for i in steps:
            l2, x2, onward = came[i]
            block = buf.at[core, l2 * NX + x2]
            wait(block, rsem.at[i])
            for j, device in onward:
                send(block, block, ssem.at[0], rsem.at[j], device)
            send(block, block, ssem.at[1], fsem.at[0], sib)

    def gather_end(buf, fsem):
        wait(buf.at[1 - core], fsem.at[0])

    def gather_sent(buf, ssem):
        wait(buf.at[0], ssem.at[0])
        wait(buf.at[0, pl.ds(0, nq - 1)], ssem.at[1])

    def cot_turn():
        fetch[0].wait()
        cotb[z, y] = cot_ref[...].astype(F32).T.astype(BF16)

    def cot_z(dz):
        own = cotb.at[z, y]
        send(own, own, s_cot.at[0], rz_cot.at[dz - 1], dev(z2=zs(dz)))

    def cot_y(dz):
        block = cotb.at[zs(NZ - dz), y]
        if dz > 0:
            wait(block, rz_cot.at[dz - 1])
        for side, dy in ((0, 1), (1, 3)):
            send(block, block, s_cot.at[1], ry_cot.at[dz, side], dev(y2=ys(dy)))

    def cot_on(dz):
        for side, dy, rows_of in ((0, 1, pl.ds(0, width // 2)), (1, 3, pl.ds(width // 2, width // 2))):
            block = cotb.at[zs(NZ - dz), ys(4 - dy)]
            wait(block, ry_cot.at[dz, side])
            part = block.at[rows_of]
            send(part, part, s_cot.at[1], ry_cot.at[dz, 2], dev(y2=ys(dy)))

    def cot_end():
        for dz in range(NZ):
            wait(cotb.at[zs(NZ - dz), ys(2)], ry_cot.at[dz, 2])

    def cot_sent():
        wait(cotb.at[0, pl.ds(0, NZ - 1)], s_cot.at[0])
        wait(cotb.at[:, pl.ds(0, 3)], s_cot.at[1])

    width = x_hbm.shape[1]

    def densify(b):
        z2 = lax.rem(b, NZ)
        y2 = b // NZ
        blocks = [adj_ref[b, s] for s in range(adj_ref.shape[1])]
        zero = jnp.zeros_like(blocks[0])
        where_to = [jnp.where(s < counts[0, b], ids[s, b], -1) for s in range(len(blocks))]
        row = pl.ds(pl.multiple_of(z2 * bs, bs), bs)
        for p in range(rows):
            total = jnp.where(where_to[0] == p, blocks[0], zero)
            for s in range(1, len(blocks)):
                total = total + jnp.where(where_to[s] == p, blocks[s], zero)
            dense[p % 2, y2, row, (p // 2) * bs : (p // 2 + 1) * bs] = total

    sides = ((0, 1), (1, 3))
    dz_order = (2, 1, 3, 0)

    def aggregate_start(feat, terms, hop, ssem, rhsem):
        def one(dy):
            y2 = lax.rem(y + dy, NY)
            total = dot(dense[0, y2], feat[0].reshape(nq * bs, -1))
            total = total + dot(dense[1, y2], feat[1].reshape(nq * bs, -1))
            terms[y2] = total.astype(BF16).reshape(terms.shape[1:])

        one(2)
        for k, dz in enumerate(dz_order):
            for side, dy in sides:
                part = terms.at[ys(2), zs(dz), pl.ds(side * half, half)]
                send(part, hop.at[k, side], ssem.at[NZ], rhsem.at[k], dev(y2=ys(dy)))
        loop(0, 3, lambda i: one(1 + 2 * i - i // 2))

    def aggregate_on(k, terms, hop, ybuf, ssem, rhsem, rysem):
        z2 = zs(dz_order[k])
        wait(hop.at[k], rhsem.at[k])
        if k >= AHEAD:
            wait(ybuf.at[k - AHEAD], ssem.at[k - AHEAD])
        for side, dy in sides:
            y2 = ys(dy)
            at = pl.ds(side * half, half)
            both = terms[y2, z2, at].astype(F32) + hop[k, side].astype(F32)
            terms[y2, z2, at] = both.astype(BF16)
            send(terms.at[y2, z2], ybuf.at[k, side], ssem.at[k], rysem.at[k], dev(y2=y2))

    def aggregate_fold(k, terms, ybuf, zsend, zrecv, ssem, rysem, rzsem):
        dz = dz_order[k]
        wait(ybuf.at[k], rysem.at[k])
        total = terms[y, zs(dz)].astype(F32) + ybuf[k, 0].astype(F32) + ybuf[k, 1].astype(F32)
        if dz:
            zsend[k] = total.astype(BF16)
            send(zsend.at[k], zrecv.at[k], ssem.at[NZ + 1], rzsem.at[0], dev(z2=zs(dz)))
        else:
            own_sum[...] = total

    def aggregate_end(zrecv, rzsem):
        wait(zrecv, rzsem.at[0])
        total = own_sum[...]
        for k in range(NZ - 1):
            total = total + zrecv[k].astype(F32)
        return total.astype(BF16)

    def aggregate_sent(hop, ybuf, zsend, ssem):
        wait(hop, ssem.at[NZ])
        wait(zsend, ssem.at[NZ + 1])
        for k in range(NZ - AHEAD, NZ):
            wait(ybuf.at[k], ssem.at[k])

    def on1(k):
        aggregate_on(k, terms1, hop1, ybuf1, s_rs1, rh_rs1, ry_rs1)

    def fold1(k):
        aggregate_fold(k, terms1, ybuf1, zsend1, zrecv1, s_rs1, ry_rs1, rz_rs1)

    upper = bs - TAIL

    def second_start():
        def one(k, dz, away):
            z2 = zs(dz)
            row = pl.ds(pl.multiple_of(z2 * bs, bs), bs)
            total = None
            for par in range(2):
                left = jnp.concatenate([dense[par, y2, row] for y2 in range(NY)], axis=0)
                part = dot(left, feat2[par].reshape(nq * bs, -1))
                total = part if total is None else total + part
            terms2[z2] = total.astype(BF16).reshape(terms2.shape[1:])
            if away:
                part = terms2.at[z2, :, pl.ds(upper, TAIL)]
                send(part, zfirst.at[dz - 1], s_rs2.at[2], rf_rs2.at[0], dev(z2=z2))
            for i, dy in enumerate((2, 1, 3)):
                part = terms2.at[z2, ys(dy), pl.ds(0, upper)]
                send(part, ybuf2.at[k, i], s_rs2.at[0], ry_rs2.at[k], dev(y2=ys(dy)))

        loop(0, NZ - 1, lambda k: one(k, 2 - k + 3 * (k // 2), True))
        one(NZ - 1, 0, False)

    def second_tail():
        wait(zfirst, rf_rs2.at[0])
        total = terms2[z, :, upper:].astype(F32)
        for i in range(NZ - 1):
            total = total + zfirst[i].astype(F32)
        ztail[...] = total.astype(BF16)
        for i, dy in enumerate((2, 1, 3)):
            send(ztail.at[ys(dy)], ytail.at[i], s_rs2.at[3], rf_rs2.at[1], dev(y2=ys(dy)))

    def second_fold(k):
        dz = dz_order[k]
        wait(ybuf2.at[k], ry_rs2.at[k])
        total = terms2[zs(dz), y, :upper].astype(F32)
        for i in range(NY - 1):
            total = total + ybuf2[k, i].astype(F32)
        if dz:
            zsend2[k] = total.astype(BF16)
            send(zsend2.at[k], zrecv2.at[k], s_rs2.at[1], rz_rs2.at[0], dev(z2=zs(dz)))
        else:
            own_sum[:upper] = total

    def second_end():
        wait(ytail, rf_rs2.at[1])
        low = ztail[y].astype(F32)
        for i in range(NY - 1):
            low = low + ytail[i].astype(F32)
        wait(zrecv2, rz_rs2.at[0])
        total = own_sum[:upper]
        for k in range(NZ - 1):
            total = total + zrecv2[k].astype(F32)
        emb_s[:upper] = total.astype(BF16)
        emb_s[upper:] = low.astype(BF16)

    def second_sent():
        wait(ybuf2, s_rs2.at[0])
        wait(zsend2, s_rs2.at[1])
        wait(zfirst, s_rs2.at[2])
        wait(ytail, s_rs2.at[3])

    two = 2 * bs

    def transposed_part(par, n, y2):
        col = pl.ds(pl.multiple_of(n * two, two), two)
        left = jnp.concatenate([cotb[z2, y2] for z2 in range(NZ)], axis=1)
        return dot(left, dense[par, y2, :, col])

    def t_near(i):
        par, n = i // (nq // 2), lax.rem(i, nq // 2)
        total = transposed_part(par, n, y) + transposed_part(par, n, ys(1))
        tnear[par, n] = total + transposed_part(par, n, ys(3))

    def t_other(n):
        total = (tnear[1 - core, n] + transposed_part(1 - core, n, ys(2))).astype(BF16)
        tsend[2 * n] = total[:, :bs]
        tsend[2 * n + 1] = total[:, bs:]
        pair = pl.ds(2 * n, 2)
        send(tsend.at[pair], trecv.at[pair], s_t.at[0], rs_t.at[n], sib)

    def t_own(n):
        total = tnear[core, n] + transposed_part(core, n, ys(2))
        wait(trecv.at[pl.ds(2 * n, 2)], rs_t.at[n])
        town[2 * n] = (total[:, :bs] + trecv[2 * n].astype(F32)).astype(BF16)
        town[2 * n + 1] = (total[:, bs:] + trecv[2 * n + 1].astype(F32)).astype(BF16)

    def t_chips():
        def one(d):
            q2 = chip_at(d)
            send(town.at[q2], tchip.at[d - 1], s_t.at[1], rc_t.at[0], (2 * q2 + core, c))

        loop(1, nq, one)

    def t_sent():
        wait(tsend, s_t.at[0])
        wait(tchip, s_t.at[1])

    def first_layer():
        mixed = aggregate_end(zrecv1, rz_rs1)
        mixed_s[...] = mixed
        pre = dot(mixed, w1_ref[...])
        pre_s[...] = pre
        hidden = (pre / (1.0 + jnp.exp(-pre))).astype(BF16)
        hidden_s[...] = hidden
        second[...] = dot(hidden, w2_ref[...]).astype(BF16)
        gather_start(second, feat2, s_ag2, r_ag2, f_ag2)
        feat2[core, q] = second[...]

    def gradients():
        wait(tchip, rc_t.at[0])
        up = town[q].astype(F32)
        for d in range(nq - 1):
            up = up + tchip[d].astype(F32)
        up = up.T.astype(BF16)
        second_grad = dot_dims(hidden_s[...], up, 0, 0) * scale
        glocal[1] = jnp.concatenate([second_grad[:width], second_grad[width:]], axis=1).astype(BF16)
        back = dot_dims(up, w2_ref[...], 1, 1)
        pre = pre_s[...]
        gate = 1.0 / (1.0 + jnp.exp(-pre))
        back_pre = (back * gate * (1.0 + pre * (1.0 - gate))).astype(BF16)
        glocal[0] = (dot_dims(mixed_s[...], back_pre, 0, 0) * scale).astype(BF16)
        send(glocal.at[1 - core], gsib, s_g.at[0], rs_g.at[0], sib)

    share = gplane.shape[1]
    place = x * NY + y

    def in_plane(d):
        m = lax.rem(place + d, NX * NY)
        return m, dev(x2=m // NY, y2=lax.rem(m, NY))

    def g_plane():
        wait(gsib, rs_g.at[0])
        both = glocal[core].astype(F32) + gsib[...].astype(F32)
        gplane[...] = both.astype(BF16).reshape(gplane.shape)

        def one(d):
            m, device = in_plane(d)
            send(gplane.at[m], gplane_r.at[d - 1], s_g.at[1], rp_g.at[0], device)

        loop(1, NX * NY, one)

    line = z * NL + l

    def g_line():
        wait(gplane_r, rp_g.at[0])
        total = gplane[place].astype(F32)
        for d in range(NX * NY - 1):
            total = total + gplane_r[d].astype(F32)
        gline[line] = total.astype(BF16)
        own = gline.at[line]

        def one(d):
            there = lax.rem(line + d, NZ * NL)
            send(own, own, s_g.at[2], rl_g.at[0], dev(l2=lax.rem(there, NL), z2=there // NL))

        loop(1, NZ * NL, one)

    def g_gather():
        wait(gline.at[pl.ds(0, NZ * NL - 1)], rl_g.at[0])
        total = gline[0].astype(F32)
        for i in range(1, NZ * NL):
            total = total + gline[i].astype(F32)
        gfin[core, place] = total.astype(BF16)
        own = gfin.at[core, place]
        loop(1, NX * NY, lambda d: send(own, own, s_g.at[3], ra_g.at[0], in_plane(d)[1]))

    def g_core():
        wait(gplane_r, ra_g.at[0])
        send(gfin.at[core], g_hbm.at[core], s_g.at[4], rf_g.at[0], sib)
        g_own_out.start()

    def g_out():
        wait(g_hbm.at[1 - core], rf_g.at[0])
        g_own_out.wait()

    def g_sent():
        wait(gsib, s_g.at[0])
        wait(gplane_r, s_g.at[1])
        wait(gline.at[pl.ds(0, NZ * NL - 1)], s_g.at[2])
        wait(gplane_r, s_g.at[3])
        wait(gfin.at[0], s_g.at[4])

    greeted(barrier)
    gather_start(x_hbm, feat1, s_ag1, r_ag1, f_ag1)
    greet(near2)
    cot_turn()
    cot_z(1)
    cot_z(3)
    cot_y(0)
    fetch[2].wait()
    loop(0, rep // 4, densify)
    greeted(near2)
    cot_z(2)
    greet(near3)
    loop(rep // 4, rep // 2, densify)
    gather_pass(feat1, s_ag1, r_ag1, f_ag1, [0])
    cot_y(1)
    cot_y(3)
    gather_pass(feat1, s_ag1, r_ag1, f_ag1, [1])
    loop(rep // 2, rep, densify)
    gather_pass(feat1, s_ag1, r_ag1, f_ag1, range(2, 7))
    cot_on(0)
    cot_y(2)
    fetch[1].wait()
    gather_end(feat1, f_ag1)
    aggregate_start(feat1, terms1, hop1, s_rs1, rh_rs1)
    cot_on(1)
    cot_on(3)
    on1(0)
    on1(1)
    on1(2)
    on1(3)
    cot_on(2)
    loop(0, nq, t_near)
    fold1(0)
    fold1(1)
    cot_end()
    loop(0, nq // 2, t_other)
    fold1(2)
    loop(0, nq // 2, t_own)
    t_chips()
    fold1(3)
    greeted(near3)
    fetch[3].wait()
    fetch[4].wait()
    first_layer()
    gather_pass(feat2, s_ag2, r_ag2, f_ag2, [0])
    gradients()
    gather_pass(feat2, s_ag2, r_ag2, f_ag2, [1])
    g_plane()
    gather_pass(feat2, s_ag2, r_ag2, f_ag2, [2, 3, 4, 5, 6])
    gather_end(feat2, f_ag2)
    second_start()
    g_line()
    second_fold(0)
    second_fold(1)
    second_tail()
    g_gather()
    second_fold(2)
    second_fold(3)
    g_core()
    second_end()
    emb_out.start()
    g_out()
    emb_out.wait()

    gather_sent(feat1, s_ag1)
    cot_sent()
    aggregate_sent(hop1, ybuf1, zsend1, s_rs1)
    gather_sent(feat2, s_ag2)
    second_sent()
    t_sent()
    g_sent()


def finish(emb_in, g_in, emb_out, g1_out, g2_out, g_s, g1_s, g2_s, sems):
    width = g1_s.shape[0]
    emb = pltpu.make_async_copy(emb_in, emb_out, sems.at[0])
    first_in = pltpu.make_async_copy(g_in.at[0], g_s.at[0], sems.at[1])
    second_in = pltpu.make_async_copy(g_in.at[1], g_s.at[1], sems.at[2])
    first_out = pltpu.make_async_copy(g1_s, g1_out, sems.at[3])
    second_out = pltpu.make_async_copy(g2_s, g2_out, sems.at[4])
    first_in.start()
    second_in.start()
    emb.start()
    first_in.wait()
    g1_s[...] = g_s[0].reshape(g1_s.shape).astype(F32)
    first_out.start()
    second_in.wait()
    grad = g_s[1].reshape(g1_s.shape).astype(F32)
    g2_s[:width] = grad[:, :width]
    g2_s[width:] = grad[:, width:]
    second_out.start()
    emb.wait()
    first_out.wait()
    second_out.wait()


def shards(nodes, node_features, adjacency, column_ids, block_counts, w1, w2, cotangent):
    rep, nq = NY * NZ, NL * NX
    bs, width = node_features.shape
    hid = w1.shape[1]
    block = (bs, width)
    turned = (width, bs)
    upper = (bs - TAIL, width)
    share = (width // (NX * NY), hid)
    vmem = pl.BlockSpec(memory_space=pltpu.VMEM)
    smem = pl.BlockSpec(memory_space=pltpu.SMEM)
    hbm = pl.BlockSpec(memory_space=pl.ANY)
    v = pltpu.VMEM
    dma = pltpu.SemaphoreType.DMA
    scratch = [
        v(adjacency.shape, BF16),
        v(w1.shape, BF16),
        v(w2.shape, BF16),
        v(block, BF16),
        v((2, NY, NZ * bs, nq * bs), BF16),
        v((2, nq) + block, BF16),
        v((2, nq) + block, BF16),
        v((NZ, NY) + turned, BF16),
        v((NY, NZ) + block, BF16),
        v((NY, NZ) + block, BF16),
        v((NZ, 2, bs // 2, width), BF16),
        v((NZ - 1, NY, TAIL, width), BF16),
        v((NY, TAIL, width), BF16),
        v((NY - 1, TAIL, width), BF16),
        v((NZ, 2) + block, BF16),
        v((NZ, NY - 1) + upper, BF16),
        v((NZ - 1,) + block, BF16),
        v((NZ - 1,) + upper, BF16),
        v((NZ - 1,) + block, BF16),
        v((NZ - 1,) + upper, BF16),
        v(block, F32),
        v(block, BF16),
        v(block, BF16),
        v((2, nq // 2, width, 2 * bs), F32),
        v((nq,) + turned, BF16),
        v((nq,) + turned, BF16),
        v((nq,) + turned, BF16),
        v((nq - 1,) + turned, BF16),
        v(block, BF16),
        v((bs, hid), BF16),
        v((bs, hid), F32),
        v((2, width, hid), BF16),
        v((width, hid), BF16),
        v((NX * NY,) + share, BF16),
        v((NX * NY - 1,) + share, BF16),
        v((NZ * NL,) + share, BF16),
        v((2, NX * NY) + share, BF16),
        pltpu.SemaphoreType.REGULAR,
        pltpu.SemaphoreType.REGULAR,
    ]
    ag = [dma((2,)), dma((7,)), dma((1,))]
    rs = [dma((NZ + 2,)), dma((NZ,)), dma((NZ,)), dma((1,))]
    scratch += ag + ag
    scratch += [dma((2,)), dma((NZ - 1,)), dma((NZ, 3))]
    scratch += rs + [dma((4,)), dma((NZ,)), dma((1,)), dma((2,))]
    scratch += [dma((2,)), dma((nq // 2,)), dma((1,))]
    scratch += [dma((5,)), dma((1,)), dma((1,)), dma((1,)), dma((1,)), dma((1,)), dma((5,)), dma((3,))]
    embedding, grads = pl.pallas_call(
        functools.partial(kernel, 1.0 / math.sqrt(nodes)),
        out_shape=(
            jax.ShapeDtypeStruct(block, BF16),
            jax.ShapeDtypeStruct((2, NX * NY) + share, BF16),
        ),
        in_specs=[smem, smem, hbm, hbm, hbm, hbm, hbm],
        out_specs=(hbm, hbm),
        scratch_shapes=scratch,
        compiler_params=pltpu.CompilerParams(
            collective_id=0, has_side_effects=True, vmem_limit_bytes=VMEM_BYTES
        ),
        name="graph_step",
    )(column_ids.T, block_counts.T, node_features, adjacency, w1, w2, cotangent)
    return pl.pallas_call(
        finish,
        out_shape=(
            jax.ShapeDtypeStruct(block, BF16),
            jax.ShapeDtypeStruct((width, hid), F32),
            jax.ShapeDtypeStruct((hid, width), F32),
        ),
        in_specs=[hbm, hbm],
        out_specs=(hbm, hbm, hbm),
        scratch_shapes=[
            v(grads.shape, BF16),
            v((width, hid), F32),
            v((hid, width), F32),
            dma((5,)),
        ],
        compiler_params=pltpu.CompilerParams(vmem_limit_bytes=VMEM_BYTES),
        name="finish",
    )(embedding, grads)


def solution(mesh):
    in_specs = (
        P(("rows", "rep"), None),
        P("rows", "rep", None, None),
        P("rows", "rep"),
        P("rows", "rep"),
        P(),
        P(),
        P(("rows", "rep"), None),
    )
    out_specs = (P(("rows", "rep"), None), P(), P())

    def run(node_features, *rest):
        body = functools.partial(shards, node_features.shape[0])
        return jax.shard_map(
            body, mesh=mesh, in_specs=in_specs, out_specs=out_specs, check_vma=False
        )(node_features, *rest)

    return run
```

```python
import functools
import math

import jax
import jax.numpy as jnp
from jax import lax
from jax.experimental import pallas as pl
from jax.experimental.pallas import tpu as pltpu
from jax.sharding import PartitionSpec as P

MESH = pl.DeviceIdType.MESH
F32 = jnp.float32
BF16 = jnp.bfloat16
VMEM_BYTES = 63 * 1024 * 1024
NL, NX, NY, NZ = 2, 4, 4, 4
AHEAD = 4
TAIL = 16


def dot(a, b):
    return jnp.dot(a, b, preferred_element_type=F32)


def dot_dims(a, b, ca, cb):
    return lax.dot_general(a, b, (((ca,), (cb,)), ((), ())), preferred_element_type=F32)


def loop(lo, hi, body):
    def step(i, carry):
        body(i)
        return carry

    lax.fori_loop(lo, hi, step, 0)


def kernel(
    scale,
    ids,
    counts,
    x_hbm,
    adj_hbm,
    w1_hbm,
    w2_hbm,
    cot_hbm,
    emb_hbm,
    g_hbm,
    adj_ref,
    w1_ref,
    w2_ref,
    cot_ref,
    dense,
    feat1,
    feat2,
    cotb,
    terms1,
    terms2,
    hop1,
    zfirst,
    ztail,
    ytail,
    ybuf1,
    ybuf2,
    zsend1,
    zsend2,
    zrecv1,
    zrecv2,
    own_sum,
    second,
    emb_s,
    tnear,
    tsend,
    trecv,
    town,
    tchip,
    mixed_s,
    hidden_s,
    pre_s,
    glocal,
    gsib,
    gplane,
    gplane_r,
    gline,
    gfin,
    near2,
    near3,
    s_ag1,
    r_ag1,
    f_ag1,
    s_ag2,
    r_ag2,
    f_ag2,
    s_cot,
    rz_cot,
    ry_cot,
    s_rs1,
    rh_rs1,
    ry_rs1,
    rz_rs1,
    s_rs2,
    ry_rs2,
    rz_rs2,
    rf_rs2,
    s_t,
    rs_t,
    rc_t,
    s_g,
    rs_g,
    rp_g,
    rl_g,
    ra_g,
    rf_g,
    s_in,
    s_out,
):
    rows, rep = 2 * NL * NX, NY * NZ
    nq = NL * NX
    bs = x_hbm.shape[0]
    half = bs // 2
    r = lax.axis_index("rows")
    c = lax.axis_index("rep")
    core = lax.rem(r, 2)
    q = r // 2
    l = q // NX
    x = lax.rem(q, NX)
    y = c // NZ
    z = lax.rem(c, NZ)
    sib = (r + 1 - 2 * core, c)

    def xs(d):
        return lax.rem(x + d, NX)

    def ys(d):
        return lax.rem(y + d, NY)

    def zs(d):
        return lax.rem(z + d, NZ)

    def dev(l2=l, x2=x, y2=y, z2=z):
        return ((l2 * NX + x2) * 2 + core, y2 * NZ + z2)

    def chip_at(d):
        return lax.rem(q + d, nq)

    def send(src, dst, ssem, rsem, device):
        pltpu.make_async_remote_copy(
            src_ref=src, dst_ref=dst, send_sem=ssem, recv_sem=rsem, device_id=device, device_id_type=MESH
        ).start()

    def wait(ref, sem):
        pltpu.make_async_copy(ref, ref, sem).wait()

    near = [
        sib,
        dev(l2=1 - l),
        dev(x2=xs(1)),
        dev(x2=xs(2)),
        dev(x2=xs(3)),
        dev(y2=ys(1)),
        dev(y2=ys(3)),
        dev(z2=zs(1)),
        dev(z2=zs(3)),
    ]

    def greet(sem):
        for device in near:
            pl.semaphore_signal(sem, inc=1, device_id=device, device_id_type=MESH)

    def greeted(sem):
        pl.semaphore_wait(sem, len(near))

    barrier = pltpu.get_barrier_semaphore()
    greet(barrier)
    emb_out = pltpu.make_async_copy(emb_s, emb_hbm, s_out.at[0])
    g_own_out = pltpu.make_async_copy(gfin.at[core], g_hbm.at[core], s_out.at[1])
    fetch = [
        pltpu.make_async_copy(src, dst, s_in.at[i])
        for i, (src, dst) in enumerate(
            [
                (cot_hbm, cot_ref),
                (x_hbm, feat1.at[core, q]),
                (adj_hbm, adj_ref),
                (w1_hbm, w1_ref),
                (w2_hbm, w2_ref),
            ]
        )
    ]
    for copy in fetch:
        copy.start()

    def gather_start(src, buf, ssem, rsem, fsem):
        to = buf.at[core, q]
        for i, device in enumerate([dev(l2=1 - l), dev(x2=xs(2)), dev(x2=xs(1)), dev(x2=xs(3))]):
            send(src, to, ssem.at[0], rsem.at[i], device)
        send(src, to, ssem.at[0], fsem.at[0], sib)

    def gather_pass(buf, ssem, rsem, fsem, steps):
        there = 1 - l
        came = [
            (there, x, [(4, dev(x2=xs(1))), (5, dev(x2=xs(3)))]),
            (l, xs(2), [(6, dev(l2=there))]),
            (l, xs(3), []),
            (l, xs(1), []),
            (there, xs(3), []),
            (there, xs(1), []),
            (there, xs(2), []),
        ]
        for i in steps:
            l2, x2, onward = came[i]
            block = buf.at[core, l2 * NX + x2]
            wait(block, rsem.at[i])
            for j, device in onward:
                send(block, block, ssem.at[0], rsem.at[j], device)
            send(block, block, ssem.at[1], fsem.at[0], sib)

    def gather_end(buf, fsem):
        wait(buf.at[1 - core], fsem.at[0])

    def gather_sent(buf, ssem):
        wait(buf.at[0], ssem.at[0])
        wait(buf.at[0, pl.ds(0, nq - 1)], ssem.at[1])

    def cot_turn():
        fetch[0].wait()
        cotb[z, y] = cot_ref[...].astype(F32).T.astype(BF16)

    def cot_z(dz):
        own = cotb.at[z, y]
        send(own, own, s_cot.at[0], rz_cot.at[dz - 1], dev(z2=zs(dz)))

    def cot_y(dz):
        block = cotb.at[zs(NZ - dz), y]
        if dz > 0:
            wait(block, rz_cot.at[dz - 1])
        for side, dy in ((0, 1), (1, 3)):
            send(block, block, s_cot.at[1], ry_cot.at[dz, side], dev(y2=ys(dy)))

    def cot_on(dz):
        for side, dy, rows_of in ((0, 1, pl.ds(0, width // 2)), (1, 3, pl.ds(width // 2, width // 2))):
            block = cotb.at[zs(NZ - dz), ys(4 - dy)]
            wait(block, ry_cot.at[dz, side])
            part = block.at[rows_of]
            send(part, part, s_cot.at[1], ry_cot.at[dz, 2], dev(y2=ys(dy)))

    def cot_end():
        for dz in range(NZ):
            wait(cotb.at[zs(NZ - dz), ys(2)], ry_cot.at[dz, 2])

    def cot_sent():
        wait(cotb.at[0, pl.ds(0, NZ - 1)], s_cot.at[0])
        wait(cotb.at[:, pl.ds(0, 3)], s_cot.at[1])

    width = x_hbm.shape[1]

    def densify(b):
        z2 = lax.rem(b, NZ)
        y2 = b // NZ
        blocks = [adj_ref[b, s] for s in range(adj_ref.shape[1])]
        zero = jnp.zeros_like(blocks[0])
        where_to = [jnp.where(s < counts[0, b], ids[s, b], -1) for s in range(len(blocks))]
        row = pl.ds(pl.multiple_of(z2 * bs, bs), bs)
        for p in range(rows):
            total = jnp.where(where_to[0] == p, blocks[0], zero)
            for s in range(1, len(blocks)):
                total = total + jnp.where(where_to[s] == p, blocks[s], zero)
            dense[p % 2, y2, row, (p // 2) * bs : (p // 2 + 1) * bs] = total

    sides = ((0, 1), (1, 3))
    dz_order = (2, 1, 3, 0)

    def aggregate_start(feat, terms, hop, ssem, rhsem):
        def one(dy):
            y2 = lax.rem(y + dy, NY)
            total = dot(dense[0, y2], feat[0].reshape(nq * bs, -1))
            total = total + dot(dense[1, y2], feat[1].reshape(nq * bs, -1))
            terms[y2] = total.astype(BF16).reshape(terms.shape[1:])

        one(2)
        for k, dz in enumerate(dz_order):
            for side, dy in sides:
                part = terms.at[ys(2), zs(dz), pl.ds(side * half, half)]
                send(part, hop.at[k, side], ssem.at[NZ], rhsem.at[k], dev(y2=ys(dy)))
        loop(0, 3, lambda i: one(1 + 2 * i - i // 2))

    def aggregate_on(k, terms, hop, ybuf, ssem, rhsem, rysem):
        z2 = zs(dz_order[k])
        wait(hop.at[k], rhsem.at[k])
        if k >= AHEAD:
            wait(ybuf.at[k - AHEAD], ssem.at[k - AHEAD])
        for side, dy in sides:
            y2 = ys(dy)
            at = pl.ds(side * half, half)
            both = terms[y2, z2, at].astype(F32) + hop[k, side].astype(F32)
            terms[y2, z2, at] = both.astype(BF16)
            send(terms.at[y2, z2], ybuf.at[k, side], ssem.at[k], rysem.at[k], dev(y2=y2))

    def aggregate_fold(k, terms, ybuf, zsend, zrecv, ssem, rysem, rzsem):
        dz = dz_order[k]
        wait(ybuf.at[k], rysem.at[k])
        total = terms[y, zs(dz)].astype(F32) + ybuf[k, 0].astype(F32) + ybuf[k, 1].astype(F32)
        if dz:
            zsend[k] = total.astype(BF16)
            send(zsend.at[k], zrecv.at[k], ssem.at[NZ + 1], rzsem.at[0], dev(z2=zs(dz)))
        else:
            own_sum[...] = total

    def aggregate_end(zrecv, rzsem):
        wait(zrecv, rzsem.at[0])
        total = own_sum[...]
        for k in range(NZ - 1):
            total = total + zrecv[k].astype(F32)
        return total.astype(BF16)

    def aggregate_sent(hop, ybuf, zsend, ssem):
        wait(hop, ssem.at[NZ])
        wait(zsend, ssem.at[NZ + 1])
        for k in range(NZ - AHEAD, NZ):
            wait(ybuf.at[k], ssem.at[k])

    def on1(k):
        aggregate_on(k, terms1, hop1, ybuf1, s_rs1, rh_rs1, ry_rs1)

    def fold1(k):
        aggregate_fold(k, terms1, ybuf1, zsend1, zrecv1, s_rs1, ry_rs1, rz_rs1)

    upper = bs - TAIL

    def second_start():
        def one(k, dz, away):
            z2 = zs(dz)
            row = pl.ds(pl.multiple_of(z2 * bs, bs), bs)
            total = None
            for par in range(2):
                left = jnp.concatenate([dense[par, y2, row] for y2 in range(NY)], axis=0)
                part = dot(left, feat2[par].reshape(nq * bs, -1))
                total = part if total is None else total + part
            terms2[z2] = total.astype(BF16).reshape(terms2.shape[1:])
            if away:
                part = terms2.at[z2, :, pl.ds(upper, TAIL)]
                send(part, zfirst.at[dz - 1], s_rs2.at[2], rf_rs2.at[0], dev(z2=z2))
            for i, dy in enumerate((2, 1, 3)):
                part = terms2.at[z2, ys(dy), pl.ds(0, upper)]
                send(part, ybuf2.at[k, i], s_rs2.at[0], ry_rs2.at[k], dev(y2=ys(dy)))

        loop(0, NZ - 1, lambda k: one(k, 2 - k + 3 * (k // 2), True))
        one(NZ - 1, 0, False)

    def second_tail():
        wait(zfirst, rf_rs2.at[0])
        total = terms2[z, :, upper:].astype(F32)
        for i in range(NZ - 1):
            total = total + zfirst[i].astype(F32)
        ztail[...] = total.astype(BF16)
        for i, dy in enumerate((2, 1, 3)):
            send(ztail.at[ys(dy)], ytail.at[i], s_rs2.at[3], rf_rs2.at[1], dev(y2=ys(dy)))

    def second_fold(k):
        dz = dz_order[k]
        wait(ybuf2.at[k], ry_rs2.at[k])
        total = terms2[zs(dz), y, :upper].astype(F32)
        for i in range(NY - 1):
            total = total + ybuf2[k, i].astype(F32)
        if dz:
            zsend2[k] = total.astype(BF16)
            send(zsend2.at[k], zrecv2.at[k], s_rs2.at[1], rz_rs2.at[0], dev(z2=zs(dz)))
        else:
            own_sum[:upper] = total

    def second_end():
        wait(ytail, rf_rs2.at[1])
        low = ztail[y].astype(F32)
        for i in range(NY - 1):
            low = low + ytail[i].astype(F32)
        wait(zrecv2, rz_rs2.at[0])
        total = own_sum[:upper]
        for k in range(NZ - 1):
            total = total + zrecv2[k].astype(F32)
        emb_s[:upper] = total.astype(BF16)
        emb_s[upper:] = low.astype(BF16)

    def second_sent():
        wait(ybuf2, s_rs2.at[0])
        wait(zsend2, s_rs2.at[1])
        wait(zfirst, s_rs2.at[2])
        wait(ytail, s_rs2.at[3])

    two = 2 * bs

    def transposed_part(par, n, y2):
        col = pl.ds(pl.multiple_of(n * two, two), two)
        left = jnp.concatenate([cotb[z2, y2] for z2 in range(NZ)], axis=1)
        return dot(left, dense[par, y2, :, col])

    def t_near(i):
        par, n = i // (nq // 2), lax.rem(i, nq // 2)
        total = transposed_part(par, n, y) + transposed_part(par, n, ys(1))
        tnear[par, n] = total + transposed_part(par, n, ys(3))

    def t_other(n):
        total = (tnear[1 - core, n] + transposed_part(1 - core, n, ys(2))).astype(BF16)
        tsend[2 * n] = total[:, :bs]
        tsend[2 * n + 1] = total[:, bs:]
        pair = pl.ds(2 * n, 2)
        send(tsend.at[pair], trecv.at[pair], s_t.at[0], rs_t.at[n], sib)

    def t_own(n):
        total = tnear[core, n] + transposed_part(core, n, ys(2))
        wait(trecv.at[pl.ds(2 * n, 2)], rs_t.at[n])
        town[2 * n] = (total[:, :bs] + trecv[2 * n].astype(F32)).astype(BF16)
        town[2 * n + 1] = (total[:, bs:] + trecv[2 * n + 1].astype(F32)).astype(BF16)

    def t_chips():
        def one(d):
            q2 = chip_at(d)
            send(town.at[q2], tchip.at[d - 1], s_t.at[1], rc_t.at[0], (2 * q2 + core, c))

        loop(1, nq, one)

    def t_sent():
        wait(tsend, s_t.at[0])
        wait(tchip, s_t.at[1])

    def first_layer():
        mixed = aggregate_end(zrecv1, rz_rs1)
        mixed_s[...] = mixed
        pre = dot(mixed, w1_ref[...])
        pre_s[...] = pre
        hidden = (pre / (1.0 + jnp.exp(-pre))).astype(BF16)
        hidden_s[...] = hidden
        second[...] = dot(hidden, w2_ref[...]).astype(BF16)
        gather_start(second, feat2, s_ag2, r_ag2, f_ag2)
        feat2[core, q] = second[...]

    def gradients():
        wait(tchip, rc_t.at[0])
        up = town[q].astype(F32)
        for d in range(nq - 1):
            up = up + tchip[d].astype(F32)
        up = up.T.astype(BF16)
        second_grad = dot_dims(hidden_s[...], up, 0, 0) * scale
        glocal[1] = jnp.concatenate([second_grad[:width], second_grad[width:]], axis=1).astype(BF16)
        back = dot_dims(up, w2_ref[...], 1, 1)
        pre = pre_s[...]
        gate = 1.0 / (1.0 + jnp.exp(-pre))
        back_pre = (back * gate * (1.0 + pre * (1.0 - gate))).astype(BF16)
        glocal[0] = (dot_dims(mixed_s[...], back_pre, 0, 0) * scale).astype(BF16)
        send(glocal.at[1 - core], gsib, s_g.at[0], rs_g.at[0], sib)

    share = gplane.shape[1]
    place = x * NY + y

    def in_plane(d):
        m = lax.rem(place + d, NX * NY)
        return m, dev(x2=m // NY, y2=lax.rem(m, NY))

    def g_plane():
        wait(gsib, rs_g.at[0])
        both = glocal[core].astype(F32) + gsib[...].astype(F32)
        gplane[...] = both.astype(BF16).reshape(gplane.shape)

        def one(d):
            m, device = in_plane(d)
            send(gplane.at[m], gplane_r.at[d - 1], s_g.at[1], rp_g.at[0], device)

        loop(1, NX * NY, one)

    line = z * NL + l

    def g_line():
        wait(gplane_r, rp_g.at[0])
        total = gplane[place].astype(F32)
        for d in range(NX * NY - 1):
            total = total + gplane_r[d].astype(F32)
        gline[line] = total.astype(BF16)
        own = gline.at[line]

        def one(d):
            there = lax.rem(line + d, NZ * NL)
            send(own, own, s_g.at[2], rl_g.at[0], dev(l2=lax.rem(there, NL), z2=there // NL))

        loop(1, NZ * NL, one)

    def g_gather():
        wait(gline.at[pl.ds(0, NZ * NL - 1)], rl_g.at[0])
        total = gline[0].astype(F32)
        for i in range(1, NZ * NL):
            total = total + gline[i].astype(F32)
        gfin[core, place] = total.astype(BF16)
        own = gfin.at[core, place]
        loop(1, NX * NY, lambda d: send(own, own, s_g.at[3], ra_g.at[0], in_plane(d)[1]))

    def g_core():
        wait(gplane_r, ra_g.at[0])
        send(gfin.at[core], g_hbm.at[core], s_g.at[4], rf_g.at[0], sib)
        g_own_out.start()

    def g_out():
        wait(g_hbm.at[1 - core], rf_g.at[0])
        g_own_out.wait()

    def g_sent():
        wait(gsib, s_g.at[0])
        wait(gplane_r, s_g.at[1])
        wait(gline.at[pl.ds(0, NZ * NL - 1)], s_g.at[2])
        wait(gplane_r, s_g.at[3])
        wait(gfin.at[0], s_g.at[4])

    greeted(barrier)
    gather_start(x_hbm, feat1, s_ag1, r_ag1, f_ag1)
    greet(near2)
    cot_turn()
    cot_z(1)
    cot_z(3)
    cot_y(0)
    fetch[2].wait()
    loop(0, rep // 4, densify)
    greeted(near2)
    cot_z(2)
    greet(near3)
    loop(rep // 4, rep // 2, densify)
    gather_pass(feat1, s_ag1, r_ag1, f_ag1, [0])
    cot_y(1)
    cot_y(3)
    gather_pass(feat1, s_ag1, r_ag1, f_ag1, [1])
    loop(rep // 2, rep, densify)
    gather_pass(feat1, s_ag1, r_ag1, f_ag1, range(2, 7))
    cot_on(0)
    cot_y(2)
    fetch[1].wait()
    gather_end(feat1, f_ag1)
    aggregate_start(feat1, terms1, hop1, s_rs1, rh_rs1)
    cot_on(1)
    cot_on(3)
    on1(0)
    on1(1)
    on1(2)
    on1(3)
    cot_on(2)
    loop(0, nq, t_near)
    fold1(0)
    fold1(1)
    cot_end()
    loop(0, nq // 2, t_other)
    fold1(2)
    loop(0, nq // 2, t_own)
    t_chips()
    fold1(3)
    greeted(near3)
    fetch[3].wait()
    fetch[4].wait()
    first_layer()
    gather_pass(feat2, s_ag2, r_ag2, f_ag2, [0])
    gradients()
    gather_pass(feat2, s_ag2, r_ag2, f_ag2, [1])
    g_plane()
    gather_pass(feat2, s_ag2, r_ag2, f_ag2, [2, 3, 4, 5, 6])
    gather_end(feat2, f_ag2)
    second_start()
    g_line()
    second_fold(0)
    g_gather()
    second_fold(1)
    second_tail()
    second_fold(2)
    second_fold(3)
    g_core()
    second_end()
    emb_out.start()
    g_out()
    emb_out.wait()

    gather_sent(feat1, s_ag1)
    cot_sent()
    aggregate_sent(hop1, ybuf1, zsend1, s_rs1)
    gather_sent(feat2, s_ag2)
    second_sent()
    t_sent()
    g_sent()


def finish(emb_in, g_in, emb_out, g1_out, g2_out, g_s, g1_s, g2_s, sems):
    width = g1_s.shape[0]
    emb = pltpu.make_async_copy(emb_in, emb_out, sems.at[0])
    first_in = pltpu.make_async_copy(g_in.at[0], g_s.at[0], sems.at[1])
    second_in = pltpu.make_async_copy(g_in.at[1], g_s.at[1], sems.at[2])
    first_out = pltpu.make_async_copy(g1_s, g1_out, sems.at[3])
    second_out = pltpu.make_async_copy(g2_s, g2_out, sems.at[4])
    first_in.start()
    second_in.start()
    emb.start()
    first_in.wait()
    g1_s[...] = g_s[0].reshape(g1_s.shape).astype(F32)
    first_out.start()
    second_in.wait()
    grad = g_s[1].reshape(g1_s.shape).astype(F32)
    g2_s[:width] = grad[:, :width]
    g2_s[width:] = grad[:, width:]
    second_out.start()
    emb.wait()
    first_out.wait()
    second_out.wait()


def shards(nodes, node_features, adjacency, column_ids, block_counts, w1, w2, cotangent):
    rep, nq = NY * NZ, NL * NX
    bs, width = node_features.shape
    hid = w1.shape[1]
    block = (bs, width)
    turned = (width, bs)
    upper = (bs - TAIL, width)
    share = (width // (NX * NY), hid)
    vmem = pl.BlockSpec(memory_space=pltpu.VMEM)
    smem = pl.BlockSpec(memory_space=pltpu.SMEM)
    hbm = pl.BlockSpec(memory_space=pl.ANY)
    v = pltpu.VMEM
    dma = pltpu.SemaphoreType.DMA
    scratch = [
        v(adjacency.shape, BF16),
        v(w1.shape, BF16),
        v(w2.shape, BF16),
        v(block, BF16),
        v((2, NY, NZ * bs, nq * bs), BF16),
        v((2, nq) + block, BF16),
        v((2, nq) + block, BF16),
        v((NZ, NY) + turned, BF16),
        v((NY, NZ) + block, BF16),
        v((NY, NZ) + block, BF16),
        v((NZ, 2, bs // 2, width), BF16),
        v((NZ - 1, NY, TAIL, width), BF16),
        v((NY, TAIL, width), BF16),
        v((NY - 1, TAIL, width), BF16),
        v((NZ, 2) + block, BF16),
        v((NZ, NY - 1) + upper, BF16),
        v((NZ - 1,) + block, BF16),
        v((NZ - 1,) + upper, BF16),
        v((NZ - 1,) + block, BF16),
        v((NZ - 1,) + upper, BF16),
        v(block, F32),
        v(block, BF16),
        v(block, BF16),
        v((2, nq // 2, width, 2 * bs), F32),
        v((nq,) + turned, BF16),
        v((nq,) + turned, BF16),
        v((nq,) + turned, BF16),
        v((nq - 1,) + turned, BF16),
        v(block, BF16),
        v((bs, hid), BF16),
        v((bs, hid), F32),
        v((2, width, hid), BF16),
        v((width, hid), BF16),
        v((NX * NY,) + share, BF16),
        v((NX * NY - 1,) + share, BF16),
        v((NZ * NL,) + share, BF16),
        v((2, NX * NY) + share, BF16),
        pltpu.SemaphoreType.REGULAR,
        pltpu.SemaphoreType.REGULAR,
    ]
    ag = [dma((2,)), dma((7,)), dma((1,))]
    rs = [dma((NZ + 2,)), dma((NZ,)), dma((NZ,)), dma((1,))]
    scratch += ag + ag
    scratch += [dma((2,)), dma((NZ - 1,)), dma((NZ, 3))]
    scratch += rs + [dma((4,)), dma((NZ,)), dma((1,)), dma((2,))]
    scratch += [dma((2,)), dma((nq // 2,)), dma((1,))]
    scratch += [dma((5,)), dma((1,)), dma((1,)), dma((1,)), dma((1,)), dma((1,)), dma((5,)), dma((3,))]
    embedding, grads = pl.pallas_call(
        functools.partial(kernel, 1.0 / math.sqrt(nodes)),
        out_shape=(
            jax.ShapeDtypeStruct(block, BF16),
            jax.ShapeDtypeStruct((2, NX * NY) + share, BF16),
        ),
        in_specs=[smem, smem, hbm, hbm, hbm, hbm, hbm],
        out_specs=(hbm, hbm),
        scratch_shapes=scratch,
        compiler_params=pltpu.CompilerParams(
            collective_id=0, has_side_effects=True, vmem_limit_bytes=VMEM_BYTES
        ),
        name="graph_step",
    )(column_ids.T, block_counts.T, node_features, adjacency, w1, w2, cotangent)
    return pl.pallas_call(
        finish,
        out_shape=(
            jax.ShapeDtypeStruct(block, BF16),
            jax.ShapeDtypeStruct((width, hid), F32),
            jax.ShapeDtypeStruct((hid, width), F32),
        ),
        in_specs=[hbm, hbm],
        out_specs=(hbm, hbm, hbm),
        scratch_shapes=[
            v(grads.shape, BF16),
            v((width, hid), F32),
            v((hid, width), F32),
            dma((5,)),
        ],
        compiler_params=pltpu.CompilerParams(vmem_limit_bytes=VMEM_BYTES),
        name="finish",
    )(embedding, grads)


def solution(mesh):
    in_specs = (
        P(("rows", "rep"), None),
        P("rows", "rep", None, None),
        P("rows", "rep"),
        P("rows", "rep"),
        P(),
        P(),
        P(("rows", "rep"), None),
    )
    out_specs = (P(("rows", "rep"), None), P(), P())

    def run(node_features, *rest):
        body = functools.partial(shards, node_features.shape[0])
        return jax.shard_map(
            body, mesh=mesh, in_specs=in_specs, out_specs=out_specs, check_vma=False
        )(node_features, *rest)

    return run
```
